256 devices in a mesh: fiber: 16 (over z, core), group: 16 (over y, x).
Axes of the slice: x: 4, y: 4, z: 8, core: 2. Of those that a mesh axis runs over, the one named last changes fastest.
Arguments:
- field_slab: float32 [512, 256, 4096], P('fiber', 'group'), may hold values from -42 to 42
- start_basis: float32 [512, 128], replicated, may hold values from -6 to 6
Outputs:
- factor: float32 [512, 128], replicated
- core_slab: float32 [128, 256, 4096], P(None, 'group', 'fiber')
The draws below stay inside these ranges and needn't reach their ends.
All inputs are finite; a program needn't handle non-finite values.
Results may differ from the reference program's by a relative error of at most 0.0003.
Values sent between devices are 32-bit elements; how exact they have to be, the bound alone decides.
A program may use at most 128 MiB of HBM per device.

```python
import math
import jax
import jax.numpy as jnp
from jax import lax

MODE = 512
RANK = 128
FIB_COLS = 256
ITERS = 2
BLOCKS = 256
WIDTH = 4096


def draw_field_slab(key, part):
    keys = jax.random.split(jax.random.fold_in(key, 7), 4)
    segments = WIDTH // FIB_COLS
    mode_pos = jnp.arange(MODE, dtype=jnp.float32)
    decay = jnp.exp(-math.log(100.0) * mode_pos / MODE)
    energy = jnp.mean(decay * decay)
    mixing = jax.random.uniform(keys[0], (MODE, MODE), jnp.float32, -math.sqrt(3.0), math.sqrt(3.0))
    mixing = mixing * (decay / jnp.sqrt(MODE * energy))[None, :]
    row_scale = jnp.exp(jax.random.uniform(keys[1], (MODE, 1, 1, 1), jnp.float32, math.log(0.5), math.log(2.0)))
    block_scale = jnp.exp(jax.random.uniform(keys[2], (MODE, BLOCKS, segments, 1), jnp.float32, math.log(0.3), math.log(3.0)))

    def one_block(index):
        pair = jax.random.split(jax.random.fold_in(keys[3], index), 2)
        latent = jax.random.truncated_normal(pair[0], -4.0, 4.0, (MODE, WIDTH), jnp.float32)
        noise = jax.random.truncated_normal(pair[1], -4.0, 4.0, (MODE, WIDTH), jnp.float32)
        mixed = jnp.dot(mixing, latent, precision=lax.Precision.HIGHEST) + 0.2 * noise
        return jnp.clip(mixed, -4.0, 4.0)
    stacked = lax.map(one_block, jnp.arange(BLOCKS))
    base = jnp.moveaxis(stacked, 0, 1).reshape(MODE, BLOCKS, segments, FIB_COLS)
    order = jnp.arange(segments, dtype=jnp.float32)[None, :] * BLOCKS + jnp.arange(BLOCKS, dtype=jnp.float32)[:, None]
    ramp = 1.0 + 0.75 * order / (BLOCKS * segments)
    values = base * row_scale * block_scale * ramp[None, :, :, None]
    return values.reshape(MODE, BLOCKS, WIDTH).astype(jnp.float32)


def centred(own_key, shape, spread, limit, held_as=jnp.bfloat16):
    result = jax.random.normal(own_key, shape, jnp.float32) * spread
    return jnp.minimum(jnp.maximum(result, -limit), limit).astype(held_as)


def setup_inputs(seed: int = 0) -> dict:
    arg_keys = jax.random.split(jax.random.key(seed), 3)
    field_slab = draw_field_slab(jax.random.fold_in(arg_keys[2], 71), 0)
    start_basis = centred(arg_keys[1], (MODE, RANK), 1.0, 6.0, jnp.float32)
    return dict(field_slab=field_slab, start_basis=start_basis)


precise = lax.Precision.HIGHEST

def orthonormal(images):
    inner_products = jnp.dot(images.T, images, precision=precise)
    cholesky_factor = jnp.linalg.cholesky(inner_products)
    return lax.linalg.triangular_solve(cholesky_factor, images, left_side=False, lower=True, transpose_a=True)

def reference(field_slab, start_basis):
    unfolded = field_slab.reshape(MODE, BLOCKS * WIDTH)
    gram_matrix = jnp.dot(unfolded, unfolded.T, precision=precise) / (BLOCKS * WIDTH)
    subspace = start_basis
    for iteration in range(ITERS):
        subspace = orthonormal(jnp.dot(gram_matrix, subspace, precision=precise))
    core_slab = jnp.einsum('mk,mbw->kbw', subspace, field_slab, precision=precise)
    return (subspace, core_slab)
```

```python
import functools
import jax
import jax.numpy as jnp
from jax import lax
from jax.experimental import pallas as pl
from jax.experimental.pallas import tpu as pltpu
from jax.sharding import PartitionSpec as P

ITERS = 2
MESH = pl.DeviceIdType.MESH
precise = lax.Precision.HIGHEST

LANES = 128


def packed_blocks(mode):
    return [(i, j) for i in range(mode // LANES) for j in range(i + 1)]


def regroup_kernel(sizes, x_ref, high_ref, low_ref, packed_ref, arrived, high, low, gram, from_core, half, from_group,
                   from_z, total, send, recv, own, out_sem, core_sem, group_send, group_recv, z_send, z_recv,
                   last_send, last_recv, last_core):
    fibers, groups, scale = sizes
    modes_each, blocks, width = x_ref.shape
    mode = modes_each * fibers
    fib_cols = width // fibers
    halves = fib_cols // LANES
    chunks = arrived.shape[0]
    me, group = lax.axis_index("fiber"), lax.axis_index("group")
    core, z = lax.rem(me, 2), lax.div(me, 2)
    zs = fibers // 2
    part_rows = from_z.shape[1]
    half_rows = half.shape[0]

    barrier = pltpu.get_barrier_semaphore()

    @pl.loop(1, fibers)
    def _(step):
        pl.semaphore_signal(barrier, inc=1, device_id={"fiber": lax.rem(me + step, fibers)}, device_id_type=MESH)

    @pl.loop(1, groups)
    def _(step):
        pl.semaphore_signal(barrier, inc=1, device_id={"group": lax.rem(group + step, groups)}, device_id_type=MESH)

    pl.semaphore_wait(barrier, fibers + groups - 2)

    def window(chunk, owner):
        row = pl.multiple_of(lax.div(chunk, halves) * 8, 8)
        col = pl.multiple_of(owner * fib_cols + lax.rem(chunk, halves) * LANES, LANES)
        return x_ref.at[:, pl.ds(row, 8), pl.ds(col, LANES)]

    def slot(chunk, source):
        return arrived.at[chunk, pl.ds(pl.multiple_of(source * modes_each, modes_each), modes_each)]

    def outgoing(chunk, step):
        target = lax.rem(me + step, fibers)
        return pltpu.make_async_remote_copy(
            src_ref=window(chunk, target), dst_ref=slot(chunk, me),
            send_sem=send.at[chunk, step], recv_sem=recv.at[chunk, step],
            device_id={"fiber": target}, device_id_type=MESH)

    def incoming(chunk, step):
        source = lax.rem(me - step + fibers, fibers)
        return pltpu.make_async_remote_copy(
            src_ref=slot(chunk, source), dst_ref=slot(chunk, source),
            send_sem=send.at[chunk, step], recv_sem=recv.at[chunk, step],
            device_id={"fiber": source}, device_id_type=MESH)

    def kept(chunk):
        return pltpu.make_async_copy(window(chunk, me), slot(chunk, me), own.at[chunk])

    @pl.loop(0, chunks)
    def _(chunk):
        kept(chunk).start()

        @pl.loop(1, fibers)
        def _(step):
            outgoing(chunk, step).start()

    gram[...] = jnp.zeros_like(gram)

    def written(chunk):
        return (pltpu.make_async_copy(high.at[chunk], high_ref.at[chunk], out_sem.at[0, chunk]),
                pltpu.make_async_copy(low.at[chunk], low_ref.at[chunk], out_sem.at[1, chunk]))

    @pl.loop(0, chunks)
    def _(chunk):
        kept(chunk).wait()

        @pl.loop(1, fibers)
        def _(step):
            incoming(chunk, step).wait_recv()

        rows_each = 64

        @pl.loop(0, mode // rows_each)
        def _(part):
            rows = pl.ds(pl.multiple_of(part * rows_each, rows_each), rows_each)
            for row in range(8):
                values = arrived[chunk, rows, row, :]
                top = values.astype(jnp.bfloat16)
                rest = (values - top.astype(jnp.float32)).astype(jnp.bfloat16)
                high[chunk, rows, row * LANES:(row + 1) * LANES] = top
                low[chunk, rows, row * LANES:(row + 1) * LANES] = rest

        for copy in written(chunk):
            copy.start()
        index = packed_blocks(mode)
        for i in range(mode // 256):
            for j in range(i + 1):
                def product(a, b):
                    return lax.dot_general(a[chunk, i * 256:(i + 1) * 256, :], b[chunk, j * 256:(j + 1) * 256, :],
                                           (((1,), (1,)), ((), ())), preferred_element_type=jnp.float32)
                tile = product(high, high) + (product(high, low) + product(low, high))
                for a in range(2):
                    for b in range(2):
                        block = (2 * i + a, 2 * j + b)
                        if block in index:
                            at = index.index(block) * LANES
                            gram[at:at + LANES, :] += tile[a * LANES:(a + 1) * LANES, b * LANES:(b + 1) * LANES]

    kept_half = pl.ds(pl.multiple_of(core * half_rows, 8), half_rows)
    other_half = pl.ds(pl.multiple_of((1 - core) * half_rows, 8), half_rows)
    swap = pltpu.make_async_remote_copy(
        src_ref=gram.at[other_half], dst_ref=from_core, send_sem=core_sem.at[0], recv_sem=core_sem.at[1],
        device_id={"fiber": 2 * z + 1 - core}, device_id_type=MESH)
    swap.start()
    swap.wait()
    half[...] = gram[kept_half, :] + from_core[...]

    def part(index):
        return pl.ds(pl.multiple_of(index * part_rows, 8), part_rows)

    def to_group(step):
        target = lax.rem(group + step, groups)
        return pltpu.make_async_remote_copy(
            src_ref=half.at[part(target)], dst_ref=from_group.at[group], send_sem=group_send.at[step],
            recv_sem=group_recv.at[step], device_id={"group": target}, device_id_type=MESH)

    def of_group(step):
        source = lax.rem(group - step + groups, groups)
        return pltpu.make_async_remote_copy(
            src_ref=from_group.at[source], dst_ref=from_group.at[source], send_sem=group_send.at[step],
            recv_sem=group_recv.at[step], device_id={"group": source}, device_id_type=MESH)

    @pl.loop(1, groups)
    def _(step):
        to_group(step).start()

    from_group[group] = half[part(group), :]

    @pl.loop(1, groups)
    def _(step):
        of_group(step).wait_recv()

    sums = from_group[0]
    for index in range(1, groups):
        sums = sums + from_group[index]
    from_z[z] = sums * scale

    def to_z(step):
        target = lax.rem(z + step, zs)
        return pltpu.make_async_remote_copy(
            src_ref=from_z.at[z], dst_ref=from_z.at[z], send_sem=z_send.at[step], recv_sem=z_recv.at[step],
            device_id={"fiber": 2 * target + core}, device_id_type=MESH)

    def of_z(step):
        source = lax.rem(z - step + zs, zs)
        return pltpu.make_async_remote_copy(
            src_ref=from_z.at[source], dst_ref=from_z.at[source], send_sem=z_send.at[step], recv_sem=z_recv.at[step],
            device_id={"fiber": 2 * source + core}, device_id_type=MESH)

    @pl.loop(1, zs)
    def _(step):
        to_z(step).start()

    @pl.loop(1, zs)
    def _(step):
        of_z(step).wait_recv()

    sums = from_z[0]
    for index in range(1, zs):
        sums = sums + from_z[index]
    total[core, group] = sums

    def share(step):
        target = lax.rem(group + step, groups)
        return pltpu.make_async_remote_copy(
            src_ref=total.at[core, group], dst_ref=total.at[core, group], send_sem=last_send.at[step],
            recv_sem=last_recv.at[step], device_id={"group": target}, device_id_type=MESH)

    def shared(step):
        source = lax.rem(group - step + groups, groups)
        return pltpu.make_async_remote_copy(
            src_ref=total.at[core, source], dst_ref=total.at[core, source], send_sem=last_send.at[step],
            recv_sem=last_recv.at[step], device_id={"group": source}, device_id_type=MESH)

    @pl.loop(1, groups)
    def _(step):
        share(step).start()

    @pl.loop(1, groups)
    def _(step):
        shared(step).wait_recv()

    give = pltpu.make_async_remote_copy(
        src_ref=total.at[core], dst_ref=total.at[core], send_sem=last_core.at[0], recv_sem=last_core.at[1],
        device_id={"fiber": 2 * z + 1 - core}, device_id_type=MESH)
    take = pltpu.make_async_remote_copy(
        src_ref=total.at[1 - core], dst_ref=total.at[1 - core], send_sem=last_core.at[0], recv_sem=last_core.at[1],
        device_id={"fiber": 2 * z + 1 - core}, device_id_type=MESH)
    give.start()
    take.wait_recv()
    packed_ref[...] = total[...]

    give.wait_send()

    @pl.loop(1, groups)
    def _(step):
        to_group(step).wait_send()
        share(step).wait_send()

    @pl.loop(1, zs)
    def _(step):
        to_z(step).wait_send()

    @pl.loop(0, chunks)
    def _(chunk):
        for copy in written(chunk):
            copy.wait()

        @pl.loop(1, fibers)
        def _(step):
            outgoing(chunk, step).wait_send()


def regroup(field_slab):
    fibers, groups = lax.axis_size("fiber"), lax.axis_size("group")
    modes_each, blocks, width = field_slab.shape
    mode, fib_cols = modes_each * fibers, width // fibers
    chunks = (blocks // 8) * (fib_cols // LANES)
    cols = 8 * LANES
    rows = len(packed_blocks(mode)) * LANES
    part_rows = rows // 2 // groups
    columns = blocks * groups * width
    f32, b16, dma = jnp.float32, jnp.bfloat16, pltpu.SemaphoreType.DMA
    return pl.pallas_call(
        functools.partial(regroup_kernel, (fibers, groups, 1.0 / columns)),
        out_shape=(jax.ShapeDtypeStruct((chunks, mode, cols), b16), jax.ShapeDtypeStruct((chunks, mode, cols), b16),
                   jax.ShapeDtypeStruct((2, groups, part_rows, LANES), f32)),
        in_specs=[pl.BlockSpec(memory_space=pl.ANY)],
        out_specs=(pl.BlockSpec(memory_space=pl.ANY), pl.BlockSpec(memory_space=pl.ANY),
                   pl.BlockSpec(memory_space=pltpu.VMEM)),
        scratch_shapes=[
            pltpu.VMEM((chunks, mode, 8, LANES), f32), pltpu.VMEM((chunks, mode, cols), b16),
            pltpu.VMEM((chunks, mode, cols), b16), pltpu.VMEM((rows, LANES), f32),
            pltpu.VMEM((rows // 2, LANES), f32), pltpu.VMEM((rows // 2, LANES), f32),
            pltpu.VMEM((groups, part_rows, LANES), f32), pltpu.VMEM((fibers // 2, part_rows, LANES), f32),
            pltpu.VMEM((2, groups, part_rows, LANES), f32),
            dma((chunks, fibers)), dma((chunks, fibers)), dma((chunks,)), dma((2, chunks)), dma((2,)),
            dma((groups,)), dma((groups,)), dma((fibers // 2,)), dma((fibers // 2,)), dma((groups,)), dma((groups,)),
            dma((2,)),
        ],
        compiler_params=pltpu.CompilerParams(collective_id=0, has_side_effects=True, vmem_limit_bytes=40 * 2**20),
        cost_estimate=pl.CostEstimate(flops=6 * mode * mode * chunks * cols, bytes_accessed=4 * mode * chunks * cols,
                                      transcendentals=0),
    )(field_slab)


def core_kernel(factor_ref, high_ref, low_ref, out_ref):
    factor = factor_ref[...].T
    top = factor.astype(jnp.bfloat16)
    rest = (factor - top.astype(jnp.float32)).astype(jnp.bfloat16)
    rank = factor.shape[0]
    both = jnp.concatenate([top, rest], axis=0)
    for row in range(8):
        cols = slice(row * LANES, (row + 1) * LANES)
        first = jnp.dot(both, high_ref[0, :, cols], preferred_element_type=jnp.float32)
        second = jnp.dot(top, low_ref[0, :, cols], preferred_element_type=jnp.float32)
        out_ref[:, row, :] = first[:rank] + (first[rank:] + second)


def make_core(factor, high, low, blocks, fib_cols):
    chunks, mode, cols = high.shape
    rank = factor.shape[1]
    halves = fib_cols // LANES
    return pl.pallas_call(
        core_kernel,
        grid=(chunks,),
        out_shape=jax.ShapeDtypeStruct((rank, blocks, fib_cols), jnp.float32),
        in_specs=[pl.BlockSpec((mode, rank), lambda c: (0, 0)), pl.BlockSpec((1, mode, cols), lambda c: (c, 0, 0)),
                  pl.BlockSpec((1, mode, cols), lambda c: (c, 0, 0))],
        out_specs=pl.BlockSpec((rank, 8, LANES), lambda c: (0, c // halves, c % halves)),
        compiler_params=pltpu.CompilerParams(vmem_limit_bytes=32 * 2**20),
        cost_estimate=pl.CostEstimate(flops=6 * mode * rank * chunks * cols, bytes_accessed=6 * mode * chunks * cols,
                                      transcendentals=0),
    )(factor, high, low)


def unpack(packed, mode):
    blocks = packed.reshape(-1, LANES, LANES)
    index = packed_blocks(mode)
    count = mode // LANES
    return jnp.block([[blocks[index.index((i, j))] if i >= j else blocks[index.index((j, i))].T for j in range(count)]
                      for i in range(count)])


def orthonormal(images):
    inner_products = jnp.dot(images.T, images, precision=precise)
    cholesky_factor = jnp.linalg.cholesky(inner_products)
    return lax.linalg.triangular_solve(
        cholesky_factor, images, left_side=False, lower=True, transpose_a=True
    )


def on_device(field_slab, start_basis):
    fib_cols = field_slab.shape[2] // lax.axis_size("fiber")
    high, low, packed = regroup(field_slab)
    gram_matrix = unpack(packed, start_basis.shape[0])
    subspace = start_basis
    for iteration in range(ITERS):
        subspace = orthonormal(jnp.dot(gram_matrix, subspace, precision=precise))
    core_slab = make_core(subspace, high, low, field_slab.shape[1], fib_cols)
    return (subspace, core_slab)


def solution(mesh):
    return jax.shard_map(
        on_device,
        mesh=mesh,
        in_specs=(P("fiber", "group", None), P()),
        out_specs=(P(), P(None, "group", "fiber")),
        check_vma=False,
    )
```

```python
import functools
import jax
import jax.numpy as jnp
from jax import lax
from jax.experimental import pallas as pl
from jax.experimental.pallas import tpu as pltpu
from jax.sharding import PartitionSpec as P

ITERS = 2
MESH = pl.DeviceIdType.MESH
precise = lax.Precision.HIGHEST
f32, b16 = jnp.float32, jnp.bfloat16

LANES = 128


def packed_blocks(mode):
    return [(i, j) for i in range(mode // LANES) for j in range(i + 1)]


def regroup_kernel(sizes, x_ref, high_ref, low_ref, packed_ref, arrived, high, low, gram, from_core, half, from_group,
                   from_z, total, send, recv, own, out_sem, core_sem, group_send, group_recv, z_send, z_recv,
                   last_send, last_recv, last_core):
    fibers, groups, scale = sizes
    modes_each, blocks, width = x_ref.shape
    mode = modes_each * fibers
    fib_cols = width // fibers
    halves = fib_cols // LANES
    chunks = arrived.shape[0]
    me, group = lax.axis_index("fiber"), lax.axis_index("group")
    core, z = lax.rem(me, 2), lax.div(me, 2)
    zs = fibers // 2
    part_rows = from_z.shape[1]
    half_rows = half.shape[0]

    barrier = pltpu.get_barrier_semaphore()

    @pl.loop(1, fibers)
    def _(step):
        pl.semaphore_signal(barrier, inc=1, device_id={"fiber": lax.rem(me + step, fibers)}, device_id_type=MESH)

    @pl.loop(1, groups)
    def _(step):
        pl.semaphore_signal(barrier, inc=1, device_id={"group": lax.rem(group + step, groups)}, device_id_type=MESH)

    pl.semaphore_wait(barrier, fibers + groups - 2)

    def window(chunk, owner):
        row = pl.multiple_of(lax.div(chunk, halves) * 8, 8)
        col = pl.multiple_of(owner * fib_cols + lax.rem(chunk, halves) * LANES, LANES)
        return x_ref.at[:, pl.ds(row, 8), pl.ds(col, LANES)]

    def slot(chunk, source):
        return arrived.at[chunk, pl.ds(pl.multiple_of(source * modes_each, modes_each), modes_each)]

    def outgoing(chunk, step):
        target = lax.rem(me + step, fibers)
        return pltpu.make_async_remote_copy(
            src_ref=window(chunk, target), dst_ref=slot(chunk, me),
            send_sem=send.at[chunk, step], recv_sem=recv.at[chunk, step],
            device_id={"fiber": target}, device_id_type=MESH)

    def incoming(chunk, step):
        source = lax.rem(me - step + fibers, fibers)
        return pltpu.make_async_remote_copy(
            src_ref=slot(chunk, source), dst_ref=slot(chunk, source),
            send_sem=send.at[chunk, step], recv_sem=recv.at[chunk, step],
            device_id={"fiber": source}, device_id_type=MESH)

    def kept(chunk):
        return pltpu.make_async_copy(window(chunk, me), slot(chunk, me), own.at[chunk])

    @pl.loop(0, chunks)
    def _(chunk):
        kept(chunk).start()

        @pl.loop(1, fibers)
        def _(step):
            outgoing(chunk, step).start()

    gram[...] = jnp.zeros_like(gram)

    def written(chunk):
        return (pltpu.make_async_copy(high.at[chunk], high_ref.at[chunk], out_sem.at[0, chunk]),
                pltpu.make_async_copy(low.at[chunk], low_ref.at[chunk], out_sem.at[1, chunk]))

    @pl.loop(0, chunks)
    def _(chunk):
        kept(chunk).wait()

        @pl.loop(1, fibers)
        def _(step):
            incoming(chunk, step).wait_recv()

        rows_each = 64

        @pl.loop(0, mode // rows_each)
        def _(part):
            rows = pl.ds(pl.multiple_of(part * rows_each, rows_each), rows_each)
            for row in range(8):
                values = arrived[chunk, rows, row, :]
                top = values.astype(jnp.bfloat16)
                rest = (values - top.astype(jnp.float32)).astype(jnp.bfloat16)
                high[chunk, rows, row * LANES:(row + 1) * LANES] = top
                low[chunk, rows, row * LANES:(row + 1) * LANES] = rest

        for copy in written(chunk):
            copy.start()
        index = packed_blocks(mode)
        for i in range(mode // 256):
            for j in range(i + 1):
                def product(a, b):
                    return lax.dot_general(a[chunk, i * 256:(i + 1) * 256, :], b[chunk, j * 256:(j + 1) * 256, :],
                                           (((1,), (1,)), ((), ())), preferred_element_type=jnp.float32)
                tile = product(high, high) + (product(high, low) + product(low, high))
                for a in range(2):
                    for b in range(2):
                        block = (2 * i + a, 2 * j + b)
                        if block in index:
                            at = index.index(block) * LANES
                            gram[at:at + LANES, :] += tile[a * LANES:(a + 1) * LANES, b * LANES:(b + 1) * LANES]

    kept_half = pl.ds(pl.multiple_of(core * half_rows, 8), half_rows)
    other_half = pl.ds(pl.multiple_of((1 - core) * half_rows, 8), half_rows)
    swap = pltpu.make_async_remote_copy(
        src_ref=gram.at[other_half], dst_ref=from_core, send_sem=core_sem.at[0], recv_sem=core_sem.at[1],
        device_id={"fiber": 2 * z + 1 - core}, device_id_type=MESH)
    swap.start()
    swap.wait()
    half[...] = gram[kept_half, :] + from_core[...]

    def part(index):
        return pl.ds(pl.multiple_of(index * part_rows, 8), part_rows)

    def to_group(step):
        target = lax.rem(group + step, groups)
        return pltpu.make_async_remote_copy(
            src_ref=half.at[part(target)], dst_ref=from_group.at[group], send_sem=group_send.at[step],
            recv_sem=group_recv.at[step], device_id={"group": target}, device_id_type=MESH)

    def of_group(step):
        source = lax.rem(group - step + groups, groups)
        return pltpu.make_async_remote_copy(
            src_ref=from_group.at[source], dst_ref=from_group.at[source], send_sem=group_send.at[step],
            recv_sem=group_recv.at[step], device_id={"group": source}, device_id_type=MESH)

    @pl.loop(1, groups)
    def _(step):
        to_group(step).start()

    from_group[group] = half[part(group), :]

    @pl.loop(1, groups)
    def _(step):
        of_group(step).wait_recv()

    sums = from_group[0]
    for index in range(1, groups):
        sums = sums + from_group[index]
    from_z[z] = sums * scale

    def to_z(step):
        target = lax.rem(z + step, zs)
        return pltpu.make_async_remote_copy(
            src_ref=from_z.at[z], dst_ref=from_z.at[z], send_sem=z_send.at[step], recv_sem=z_recv.at[step],
            device_id={"fiber": 2 * target + core}, device_id_type=MESH)

    def of_z(step):
        source = lax.rem(z - step + zs, zs)
        return pltpu.make_async_remote_copy(
            src_ref=from_z.at[source], dst_ref=from_z.at[source], send_sem=z_send.at[step], recv_sem=z_recv.at[step],
            device_id={"fiber": 2 * source + core}, device_id_type=MESH)

    @pl.loop(1, zs)
    def _(step):
        to_z(step).start()

    @pl.loop(1, zs)
    def _(step):
        of_z(step).wait_recv()

    sums = from_z[0]
    for index in range(1, zs):
        sums = sums + from_z[index]
    total[core, group] = sums

    def share(step):
        target = lax.rem(group + step, groups)
        return pltpu.make_async_remote_copy(
            src_ref=total.at[core, group], dst_ref=total.at[core, group], send_sem=last_send.at[step],
            recv_sem=last_recv.at[step], device_id={"group": target}, device_id_type=MESH)

    def shared(step):
        source = lax.rem(group - step + groups, groups)
        return pltpu.make_async_remote_copy(
            src_ref=total.at[core, source], dst_ref=total.at[core, source], send_sem=last_send.at[step],
            recv_sem=last_recv.at[step], device_id={"group": source}, device_id_type=MESH)

    @pl.loop(1, groups)
    def _(step):
        share(step).start()

    @pl.loop(1, groups)
    def _(step):
        shared(step).wait_recv()

    give = pltpu.make_async_remote_copy(
        src_ref=total.at[core], dst_ref=total.at[core], send_sem=last_core.at[0], recv_sem=last_core.at[1],
        device_id={"fiber": 2 * z + 1 - core}, device_id_type=MESH)
    take = pltpu.make_async_remote_copy(
        src_ref=total.at[1 - core], dst_ref=total.at[1 - core], send_sem=last_core.at[0], recv_sem=last_core.at[1],
        device_id={"fiber": 2 * z + 1 - core}, device_id_type=MESH)
    give.start()
    take.wait_recv()
    packed_ref[...] = total[...]

    give.wait_send()

    @pl.loop(1, groups)
    def _(step):
        to_group(step).wait_send()
        share(step).wait_send()

    @pl.loop(1, zs)
    def _(step):
        to_z(step).wait_send()

    @pl.loop(0, chunks)
    def _(chunk):
        for copy in written(chunk):
            copy.wait()

        @pl.loop(1, fibers)
        def _(step):
            outgoing(chunk, step).wait_send()


def regroup(field_slab):
    fibers, groups = lax.axis_size("fiber"), lax.axis_size("group")
    modes_each, blocks, width = field_slab.shape
    mode, fib_cols = modes_each * fibers, width // fibers
    chunks = (blocks // 8) * (fib_cols // LANES)
    cols = 8 * LANES
    rows = len(packed_blocks(mode)) * LANES
    part_rows = rows // 2 // groups
    columns = blocks * groups * width
    dma = pltpu.SemaphoreType.DMA
    return pl.pallas_call(
        functools.partial(regroup_kernel, (fibers, groups, 1.0 / columns)),
        out_shape=(jax.ShapeDtypeStruct((chunks, mode, cols), b16), jax.ShapeDtypeStruct((chunks, mode, cols), b16),
                   jax.ShapeDtypeStruct((2, groups, part_rows, LANES), f32)),
        in_specs=[pl.BlockSpec(memory_space=pl.ANY)],
        out_specs=(pl.BlockSpec(memory_space=pl.ANY), pl.BlockSpec(memory_space=pl.ANY),
                   pl.BlockSpec(memory_space=pltpu.VMEM)),
        scratch_shapes=[
            pltpu.VMEM((chunks, mode, 8, LANES), f32), pltpu.VMEM((chunks, mode, cols), b16),
            pltpu.VMEM((chunks, mode, cols), b16), pltpu.VMEM((rows, LANES), f32),
            pltpu.VMEM((rows // 2, LANES), f32), pltpu.VMEM((rows // 2, LANES), f32),
            pltpu.VMEM((groups, part_rows, LANES), f32), pltpu.VMEM((fibers // 2, part_rows, LANES), f32),
            pltpu.VMEM((2, groups, part_rows, LANES), f32),
            dma((chunks, fibers)), dma((chunks, fibers)), dma((chunks,)), dma((2, chunks)), dma((2,)),
            dma((groups,)), dma((groups,)), dma((fibers // 2,)), dma((fibers // 2,)), dma((groups,)), dma((groups,)),
            dma((2,)),
        ],
        compiler_params=pltpu.CompilerParams(collective_id=0, has_side_effects=True, vmem_limit_bytes=40 * 2**20),
        cost_estimate=pl.CostEstimate(flops=6 * mode * mode * chunks * cols, bytes_accessed=4 * mode * chunks * cols,
                                      transcendentals=0),
    )(field_slab)


def pieces(values):
    top = values.astype(b16)
    rest = values - top.astype(f32)
    middle = rest.astype(b16)
    return top, middle, (rest - middle.astype(f32)).astype(b16)

def outer(rows):
    t, m, l = pieces(rows)
    left = jnp.concatenate([t, t, m, m, t, l], axis=0)[:, :LANES]
    right = jnp.concatenate([t, m, t, m, l, t], axis=0)
    return lax.dot_general(left, right, (((0,), (0,)), ((), ())), preferred_element_type=f32)

def inverse_lower(wide, rank, panel):
    ids = lax.broadcasted_iota(jnp.int32, (panel, LANES), 0)
    for start in range(0, rank, panel):
        rows = wide[start:start + panel, :]
        diag = [jnp.broadcast_to(rows[:, start + k:start + k + 1], (panel, LANES)) for k in range(panel)]
        parts = [rows[:, :LANES], rows[:, LANES:]]
        for j in range(panel):
            scale = lax.rsqrt(diag[j][j:j + 1, :])
            below = ids > j
            factor = jnp.where(below, diag[j] * scale, 0.0)
            keep = jnp.where(ids == j, scale, 1.0)
            def step(block):
                pivot = block[j:j + 1, :] * scale
                return block * keep - factor * pivot
            for k in range(j + 1, panel):
                diag[k] = diag[k] - factor * (diag[k][j:j + 1, :] * scale)
            parts = [step(block) for block in parts]
        rows = jnp.concatenate(parts, axis=1)
        wide[start:start + panel, :] = rows
        if start + panel < rank:
            wide[start + panel:, :] = wide[start + panel:, :] - outer(rows)[start + panel:, :]

def finish_kernel(iters, panel, packed_ref, basis_ref, high_ref, low_ref, factor_ref, core_ref, high, low, gram, wide,
                  made, in_sem, out_sem):
    mode, rank = basis_ref.shape
    chunks = high.shape[0]
    fetch = [(pltpu.make_async_copy(high_ref.at[q], high.at[q], in_sem.at[0, q]),
              pltpu.make_async_copy(low_ref.at[q], low.at[q], in_sem.at[1, q])) for q in range(chunks)]
    for pair in fetch:
        for copy in pair:
            copy.start()
    for at, (i, j) in enumerate(packed_blocks(mode)):
        block = packed_ref[at * LANES:(at + 1) * LANES, :]
        gram[i * LANES:(i + 1) * LANES, j * LANES:(j + 1) * LANES] = block
        if i != j:
            gram[j * LANES:(j + 1) * LANES, i * LANES:(i + 1) * LANES] = block.T
    subspace = basis_ref[...].T
    identity = jnp.where(lax.broadcasted_iota(jnp.int32, (rank, rank), 0)
                         == lax.broadcasted_iota(jnp.int32, (rank, rank), 1), 1.0, 0.0).astype(f32)
    for iteration in range(iters):
        images = jnp.dot(subspace, gram[...], precision=precise, preferred_element_type=f32)
        inner = lax.dot_general(images, images, (((1,), (1,)), ((), ())), precision=precise, preferred_element_type=f32)
        wide[:, :LANES] = inner
        wide[:, LANES:] = identity
        inverse_lower(wide, rank, panel)
        subspace = jnp.dot(wide[:, LANES:], images, precision=precise, preferred_element_type=f32)
    factor_ref[...] = subspace.T
    top = subspace.astype(b16)
    rest = (subspace - top.astype(f32)).astype(b16)
    both = jnp.concatenate([top, rest], axis=0)
    halves = core_ref.shape[2] // LANES
    copies = []
    for q in range(chunks):
        for copy in fetch[q]:
            copy.wait()
        for pair in range(4):
            cols = slice(2 * pair * LANES, 2 * (pair + 1) * LANES)
            first = jnp.dot(both, high[q, :, cols], preferred_element_type=f32)
            second = jnp.dot(top, low[q, :, cols], preferred_element_type=f32)
            value = first[:rank] + (first[rank:] + second)
            made[q, :, 2 * pair, :] = value[:, :LANES]
            made[q, :, 2 * pair + 1, :] = value[:, LANES:]
        row, col = q // halves * 8, q % halves * LANES
        copy = pltpu.make_async_copy(made.at[q], core_ref.at[:, row:row + 8, col:col + LANES], out_sem.at[q])
        copy.start()
        copies.append(copy)
    for copy in copies:
        copy.wait()

def finish(packed, basis, high, low, blocks, fib_cols, iters=ITERS, panel=16):
    mode, rank = basis.shape
    chunks, _, cols = high.shape
    vmem, any_ = pl.BlockSpec(memory_space=pltpu.VMEM), pl.BlockSpec(memory_space=pl.ANY)
    return pl.pallas_call(
        functools.partial(finish_kernel, iters, panel),
        out_shape=(jax.ShapeDtypeStruct((mode, rank), f32), jax.ShapeDtypeStruct((rank, blocks, fib_cols), f32)),
        in_specs=[vmem, vmem, any_, any_],
        out_specs=(vmem, any_),
        scratch_shapes=[pltpu.VMEM((chunks, mode, cols), b16), pltpu.VMEM((chunks, mode, cols), b16),
                        pltpu.VMEM((mode, mode), f32), pltpu.VMEM((rank, 2 * LANES), f32),
                        pltpu.VMEM((chunks, rank, 8, LANES), f32),
                        pltpu.SemaphoreType.DMA((2, chunks)), pltpu.SemaphoreType.DMA((chunks,))],
        compiler_params=pltpu.CompilerParams(vmem_limit_bytes=32 * 2**20),
        cost_estimate=pl.CostEstimate(flops=6 * mode * rank * chunks * cols, bytes_accessed=6 * mode * chunks * cols,
                                      transcendentals=0),
    )(packed, basis, high, low)


def on_device(field_slab, start_basis):
    fib_cols = field_slab.shape[2] // lax.axis_size("fiber")
    high, low, packed = regroup(field_slab)
    return finish(packed.reshape(-1, LANES), start_basis, high, low, field_slab.shape[1], fib_cols)


def solution(mesh):
    return jax.shard_map(
        on_device,
        mesh=mesh,
        in_specs=(P("fiber", "group", None), P()),
        out_specs=(P(), P(None, "group", "fiber")),
        check_vma=False,
    )
```

```python
import functools
import jax
import jax.numpy as jnp
from jax import lax
from jax.experimental import pallas as pl
from jax.experimental.pallas import tpu as pltpu
from jax.sharding import PartitionSpec as P

ITERS = 2
MESH = pl.DeviceIdType.MESH
precise = lax.Precision.HIGHEST
f32, b16 = jnp.float32, jnp.bfloat16

LANES = 128


def packed_blocks(mode):
    return [(i, j) for i in range(mode // LANES) for j in range(i + 1)]


def regroup_kernel(sizes, x_ref, high_ref, low_ref, packed_ref, arrived, high, low, gram, from_core, half, from_group,
                   from_z, total, send, recv, own, out_sem, core_sem, group_send, group_recv, z_send, z_recv,
                   last_send, last_recv, last_core):
    fibers, groups, scale = sizes
    modes_each, blocks, width = x_ref.shape
    mode = modes_each * fibers
    fib_cols = width // fibers
    halves = fib_cols // LANES
    chunks = arrived.shape[0]
    me, group = lax.axis_index("fiber"), lax.axis_index("group")
    core, z = lax.rem(me, 2), lax.div(me, 2)
    zs = fibers // 2
    part_rows = from_z.shape[1]
    half_rows = half.shape[0]

    barrier = pltpu.get_barrier_semaphore()

    @pl.loop(1, fibers)
    def _(step):
        pl.semaphore_signal(barrier, inc=1, device_id={"fiber": lax.rem(me + step, fibers)}, device_id_type=MESH)

    @pl.loop(1, groups)
    def _(step):
        pl.semaphore_signal(barrier, inc=1, device_id={"group": lax.rem(group + step, groups)}, device_id_type=MESH)

    pl.semaphore_wait(barrier, fibers + groups - 2)

    def window(chunk, owner):
        row = pl.multiple_of(lax.div(chunk, halves) * 8, 8)
        col = pl.multiple_of(owner * fib_cols + lax.rem(chunk, halves) * LANES, LANES)
        return x_ref.at[:, pl.ds(row, 8), pl.ds(col, LANES)]

    def slot(chunk, source):
        return arrived.at[chunk, pl.ds(pl.multiple_of(source * modes_each, modes_each), modes_each)]

    def outgoing(chunk, step):
        target = lax.rem(me + step, fibers)
        return pltpu.make_async_remote_copy(
            src_ref=window(chunk, target), dst_ref=slot(chunk, me),
            send_sem=send.at[chunk, step], recv_sem=recv.at[chunk, step],
            device_id={"fiber": target}, device_id_type=MESH)

    def incoming(chunk, step):
        source = lax.rem(me - step + fibers, fibers)
        return pltpu.make_async_remote_copy(
            src_ref=slot(chunk, source), dst_ref=slot(chunk, source),
            send_sem=send.at[chunk, step], recv_sem=recv.at[chunk, step],
            device_id={"fiber": source}, device_id_type=MESH)

    def kept(chunk):
        return pltpu.make_async_copy(window(chunk, me), slot(chunk, me), own.at[chunk])

    @pl.loop(0, chunks)
    def _(chunk):
        kept(chunk).start()

        @pl.loop(1, fibers)
        def _(step):
            outgoing(chunk, step).start()

    gram[...] = jnp.zeros_like(gram)

    def written(chunk):
        return (pltpu.make_async_copy(high.at[chunk], high_ref.at[chunk], out_sem.at[0, chunk]),
                pltpu.make_async_copy(low.at[chunk], low_ref.at[chunk], out_sem.at[1, chunk]))

    @pl.loop(0, chunks)
    def _(chunk):
        kept(chunk).wait()

        @pl.loop(1, fibers)
        def _(step):
            incoming(chunk, step).wait_recv()

        rows_each = 64

        @pl.loop(0, mode // rows_each)
        def _(part):
            rows = pl.ds(pl.multiple_of(part * rows_each, rows_each), rows_each)
            values = arrived[chunk, rows].reshape(rows_each, 8 * LANES)
            top = values.astype(jnp.bfloat16)
            high[chunk, rows, :] = top
            low[chunk, rows, :] = (values - top.astype(jnp.float32)).astype(jnp.bfloat16)

        for copy in written(chunk):
            copy.start()
        index = packed_blocks(mode)
        for i in range(mode // 256):
            for j in range(i + 1):
                def product(a, b):
                    return lax.dot_general(a[chunk, i * 256:(i + 1) * 256, :], b[chunk, j * 256:(j + 1) * 256, :],
                                           (((1,), (1,)), ((), ())), preferred_element_type=jnp.float32)
                tile = product(high, high) + (product(high, low) + product(low, high))
                for a in range(2):
                    for b in range(2):
                        block = (2 * i + a, 2 * j + b)
                        if block in index:
                            at = index.index(block) * LANES
                            gram[at:at + LANES, :] += tile[a * LANES:(a + 1) * LANES, b * LANES:(b + 1) * LANES]

    kept_half = pl.ds(pl.multiple_of(core * half_rows, 8), half_rows)
    other_half = pl.ds(pl.multiple_of((1 - core) * half_rows, 8), half_rows)
    swap = pltpu.make_async_remote_copy(
        src_ref=gram.at[other_half], dst_ref=from_core, send_sem=core_sem.at[0], recv_sem=core_sem.at[1],
        device_id={"fiber": 2 * z + 1 - core}, device_id_type=MESH)
    swap.start()
    swap.wait()
    half[...] = gram[kept_half, :] + from_core[...]

    def part(index):
        return pl.ds(pl.multiple_of(index * part_rows, 8), part_rows)

    def to_group(step):
        target = lax.rem(group + step, groups)
        return pltpu.make_async_remote_copy(
            src_ref=half.at[part(target)], dst_ref=from_group.at[group], send_sem=group_send.at[step],
            recv_sem=group_recv.at[step], device_id={"group": target}, device_id_type=MESH)

    def of_group(step):
        source = lax.rem(group - step + groups, groups)
        return pltpu.make_async_remote_copy(
            src_ref=from_group.at[source], dst_ref=from_group.at[source], send_sem=group_send.at[step],
            recv_sem=group_recv.at[step], device_id={"group": source}, device_id_type=MESH)

    @pl.loop(1, groups)
    def _(step):
        to_group(step).start()

    from_group[group] = half[part(group), :]

    @pl.loop(1, groups)
    def _(step):
        of_group(step).wait_recv()

    sums = from_group[0]
    for index in range(1, groups):
        sums = sums + from_group[index]
    from_z[z] = sums * scale

    def to_z(step):
        target = lax.rem(z + step, zs)
        return pltpu.make_async_remote_copy(
            src_ref=from_z.at[z], dst_ref=from_z.at[z], send_sem=z_send.at[step], recv_sem=z_recv.at[step],
            device_id={"fiber": 2 * target + core}, device_id_type=MESH)

    def of_z(step):
        source = lax.rem(z - step + zs, zs)
        return pltpu.make_async_remote_copy(
            src_ref=from_z.at[source], dst_ref=from_z.at[source], send_sem=z_send.at[step], recv_sem=z_recv.at[step],
            device_id={"fiber": 2 * source + core}, device_id_type=MESH)

    @pl.loop(1, zs)
    def _(step):
        to_z(step).start()

    @pl.loop(1, zs)
    def _(step):
        of_z(step).wait_recv()

    sums = from_z[0]
    for index in range(1, zs):
        sums = sums + from_z[index]
    total[core, group] = sums

    def share(step):
        target = lax.rem(group + step, groups)
        return pltpu.make_async_remote_copy(
            src_ref=total.at[core, group], dst_ref=total.at[core, group], send_sem=last_send.at[step],
            recv_sem=last_recv.at[step], device_id={"group": target}, device_id_type=MESH)

    def shared(step):
        source = lax.rem(group - step + groups, groups)
        return pltpu.make_async_remote_copy(
            src_ref=total.at[core, source], dst_ref=total.at[core, source], send_sem=last_send.at[step],
            recv_sem=last_recv.at[step], device_id={"group": source}, device_id_type=MESH)

    @pl.loop(1, groups)
    def _(step):
        share(step).start()

    @pl.loop(1, groups)
    def _(step):
        shared(step).wait_recv()

    give = pltpu.make_async_remote_copy(
        src_ref=total.at[core], dst_ref=total.at[core], send_sem=last_core.at[0], recv_sem=last_core.at[1],
        device_id={"fiber": 2 * z + 1 - core}, device_id_type=MESH)
    take = pltpu.make_async_remote_copy(
        src_ref=total.at[1 - core], dst_ref=total.at[1 - core], send_sem=last_core.at[0], recv_sem=last_core.at[1],
        device_id={"fiber": 2 * z + 1 - core}, device_id_type=MESH)
    give.start()
    take.wait_recv()
    packed_ref[...] = total[...]

    give.wait_send()

    @pl.loop(1, groups)
    def _(step):
        to_group(step).wait_send()
        share(step).wait_send()

    @pl.loop(1, zs)
    def _(step):
        to_z(step).wait_send()

    @pl.loop(0, chunks)
    def _(chunk):
        for copy in written(chunk):
            copy.wait()

        @pl.loop(1, fibers)
        def _(step):
            outgoing(chunk, step).wait_send()


def regroup(field_slab):
    fibers, groups = lax.axis_size("fiber"), lax.axis_size("group")
    modes_each, blocks, width = field_slab.shape
    mode, fib_cols = modes_each * fibers, width // fibers
    chunks = (blocks // 8) * (fib_cols // LANES)
    cols = 8 * LANES
    rows = len(packed_blocks(mode)) * LANES
    part_rows = rows // 2 // groups
    columns = blocks * groups * width
    dma = pltpu.SemaphoreType.DMA
    return pl.pallas_call(
        functools.partial(regroup_kernel, (fibers, groups, 1.0 / columns)),
        out_shape=(jax.ShapeDtypeStruct((chunks, mode, cols), b16), jax.ShapeDtypeStruct((chunks, mode, cols), b16),
                   jax.ShapeDtypeStruct((2, groups, part_rows, LANES), f32)),
        in_specs=[pl.BlockSpec(memory_space=pl.ANY)],
        out_specs=(pl.BlockSpec(memory_space=pl.ANY), pl.BlockSpec(memory_space=pl.ANY),
                   pl.BlockSpec(memory_space=pltpu.VMEM)),
        scratch_shapes=[
            pltpu.VMEM((chunks, mode, 8, LANES), f32), pltpu.VMEM((chunks, mode, cols), b16),
            pltpu.VMEM((chunks, mode, cols), b16), pltpu.VMEM((rows, LANES), f32),
            pltpu.VMEM((rows // 2, LANES), f32), pltpu.VMEM((rows // 2, LANES), f32),
            pltpu.VMEM((groups, part_rows, LANES), f32), pltpu.VMEM((fibers // 2, part_rows, LANES), f32),
            pltpu.VMEM((2, groups, part_rows, LANES), f32),
            dma((chunks, fibers)), dma((chunks, fibers)), dma((chunks,)), dma((2, chunks)), dma((2,)),
            dma((groups,)), dma((groups,)), dma((fibers // 2,)), dma((fibers // 2,)), dma((groups,)), dma((groups,)),
            dma((2,)),
        ],
        compiler_params=pltpu.CompilerParams(collective_id=0, has_side_effects=True, vmem_limit_bytes=40 * 2**20),
        cost_estimate=pl.CostEstimate(flops=6 * mode * mode * chunks * cols, bytes_accessed=4 * mode * chunks * cols,
                                      transcendentals=0),
    )(field_slab)


def pieces(values):
    top = values.astype(b16)
    rest = values - top.astype(f32)
    middle = rest.astype(b16)
    return top, middle, (rest - middle.astype(f32)).astype(b16)

def outer(rows):
    t, m, l = pieces(rows)
    left = jnp.concatenate([t, t, m, m, t, l], axis=0)[:, :LANES]
    right = jnp.concatenate([t, m, t, m, l, t], axis=0)
    return lax.dot_general(left, right, (((0,), (0,)), ((), ())), preferred_element_type=f32)

def inverse_lower(wide, rank, panel):
    ids = lax.broadcasted_iota(jnp.int32, (panel, LANES), 0)
    for start in range(0, rank, panel):
        rows = wide[start:start + panel, :]
        diag = [jnp.broadcast_to(rows[:, start + k:start + k + 1], (panel, LANES)) for k in range(panel)]
        parts = [rows[:, :LANES], rows[:, LANES:]]
        for j in range(panel):
            scale = lax.rsqrt(diag[j][j:j + 1, :])
            below = ids > j
            factor = jnp.where(below, diag[j] * scale, 0.0)
            keep = jnp.where(ids == j, scale, 1.0)
            def step(block):
                pivot = block[j:j + 1, :] * scale
                return block * keep - factor * pivot
            for k in range(j + 1, panel):
                diag[k] = diag[k] - factor * (diag[k][j:j + 1, :] * scale)
            parts = [step(block) for block in parts]
        rows = jnp.concatenate(parts, axis=1)
        wide[start:start + panel, :] = rows
        if start + panel < rank:
            wide[start + panel:, :] = wide[start + panel:, :] - outer(rows)[start + panel:, :]

def finish_kernel(iters, panel, packed_ref, basis_ref, high_ref, low_ref, factor_ref, core_ref, high, low, gram, wide,
                  made, in_sem, out_sem):
    mode, rank = basis_ref.shape
    chunks = high.shape[0]
    fetch = [(pltpu.make_async_copy(high_ref.at[q], high.at[q], in_sem.at[0, q]),
              pltpu.make_async_copy(low_ref.at[q], low.at[q], in_sem.at[1, q])) for q in range(chunks)]
    for pair in fetch:
        for copy in pair:
            copy.start()
    for at, (i, j) in enumerate(packed_blocks(mode)):
        block = packed_ref[at * LANES:(at + 1) * LANES, :]
        gram[i * LANES:(i + 1) * LANES, j * LANES:(j + 1) * LANES] = block
        if i != j:
            gram[j * LANES:(j + 1) * LANES, i * LANES:(i + 1) * LANES] = block.T
    subspace = basis_ref[...].T
    identity = jnp.where(lax.broadcasted_iota(jnp.int32, (rank, rank), 0)
                         == lax.broadcasted_iota(jnp.int32, (rank, rank), 1), 1.0, 0.0).astype(f32)
    for iteration in range(iters):
        images = jnp.dot(subspace, gram[...], precision=precise, preferred_element_type=f32)
        inner = lax.dot_general(images, images, (((1,), (1,)), ((), ())), precision=precise, preferred_element_type=f32)
        wide[:, :LANES] = inner
        wide[:, LANES:] = identity
        inverse_lower(wide, rank, panel)
        subspace = jnp.dot(wide[:, LANES:], images, precision=precise, preferred_element_type=f32)
    factor_ref[...] = subspace.T
    top = subspace.astype(b16)
    rest = (subspace - top.astype(f32)).astype(b16)
    both = jnp.concatenate([top, rest], axis=0)
    halves = core_ref.shape[2] // LANES
    copies = []
    for q in range(chunks):
        for copy in fetch[q]:
            copy.wait()
        first = jnp.dot(both, high[q], preferred_element_type=f32)
        second = jnp.dot(top, low[q], preferred_element_type=f32)
        made[q] = (first[:rank] + (first[rank:] + second)).reshape(rank, 8, LANES)
        row, col = q // halves * 8, q % halves * LANES
        copy = pltpu.make_async_copy(made.at[q], core_ref.at[:, row:row + 8, col:col + LANES], out_sem.at[q])
        copy.start()
        copies.append(copy)
    for copy in copies:
        copy.wait()

def finish(packed, basis, high, low, blocks, fib_cols, iters=ITERS, panel=16):
    mode, rank = basis.shape
    chunks, _, cols = high.shape
    vmem, any_ = pl.BlockSpec(memory_space=pltpu.VMEM), pl.BlockSpec(memory_space=pl.ANY)
    return pl.pallas_call(
        functools.partial(finish_kernel, iters, panel),
        out_shape=(jax.ShapeDtypeStruct((mode, rank), f32), jax.ShapeDtypeStruct((rank, blocks, fib_cols), f32)),
        in_specs=[vmem, vmem, any_, any_],
        out_specs=(vmem, any_),
        scratch_shapes=[pltpu.VMEM((chunks, mode, cols), b16), pltpu.VMEM((chunks, mode, cols), b16),
                        pltpu.VMEM((mode, mode), f32), pltpu.VMEM((rank, 2 * LANES), f32),
                        pltpu.VMEM((chunks, rank, 8, LANES), f32),
                        pltpu.SemaphoreType.DMA((2, chunks)), pltpu.SemaphoreType.DMA((chunks,))],
        compiler_params=pltpu.CompilerParams(vmem_limit_bytes=32 * 2**20),
        cost_estimate=pl.CostEstimate(flops=6 * mode * rank * chunks * cols, bytes_accessed=6 * mode * chunks * cols,
                                      transcendentals=0),
    )(packed, basis, high, low)


def on_device(field_slab, start_basis):
    fib_cols = field_slab.shape[2] // lax.axis_size("fiber")
    high, low, packed = regroup(field_slab)
    return finish(packed.reshape(-1, LANES), start_basis, high, low, field_slab.shape[1], fib_cols)


def solution(mesh):
    return jax.shard_map(
        on_device,
        mesh=mesh,
        in_specs=(P("fiber", "group", None), P()),
        out_specs=(P(), P(None, "group", "fiber")),
        check_vma=False,
    )
```

```python
import functools
import jax
import jax.numpy as jnp
from jax import lax
from jax.experimental import pallas as pl
from jax.experimental.pallas import tpu as pltpu
from jax.sharding import PartitionSpec as P

ITERS = 2
MESH = pl.DeviceIdType.MESH
precise = lax.Precision.HIGHEST
f32, b16 = jnp.float32, jnp.bfloat16

LANES = 128


def packed_blocks(mode):
    return [(i, j) for i in range(mode // LANES) for j in range(i + 1)]


def regroup_kernel(sizes, x_ref, high_ref, low_ref, packed_ref, arrived, high, low, gram, from_core, half, from_group,
                   from_z, total, send, recv, own, out_sem, core_sem, group_send, group_recv, z_send, z_recv,
                   last_send, last_recv, last_core):
    fibers, groups, scale = sizes
    modes_each, blocks, width = x_ref.shape
    mode = modes_each * fibers
    fib_cols = width // fibers
    halves = fib_cols // LANES
    chunks = arrived.shape[0]
    me, group = lax.axis_index("fiber"), lax.axis_index("group")
    core, z = lax.rem(me, 2), lax.div(me, 2)
    zs = fibers // 2
    part_rows = from_z.shape[1]
    half_rows = half.shape[0]

    barrier = pltpu.get_barrier_semaphore()

    def far_first(count):
        def run(body):
            @pl.loop(0, count - 1)
            def _(index):
                body(lax.rem(index + count // 2 - 1, count - 1) + 1)
        return run

    @far_first(groups)
    def _(step):
        pl.semaphore_signal(barrier, inc=1, device_id={"group": lax.rem(group + step, groups)}, device_id_type=MESH)

    @far_first(fibers)
    def _(step):
        pl.semaphore_signal(barrier, inc=1, device_id={"fiber": lax.rem(me + step, fibers)}, device_id_type=MESH)

    pl.semaphore_wait(barrier, fibers + groups - 2)

    def window(chunk, owner):
        row = pl.multiple_of(lax.div(chunk, halves) * 8, 8)
        col = pl.multiple_of(owner * fib_cols + lax.rem(chunk, halves) * LANES, LANES)
        return x_ref.at[:, pl.ds(row, 8), pl.ds(col, LANES)]

    def slot(chunk, source):
        return arrived.at[chunk, pl.ds(pl.multiple_of(source * modes_each, modes_each), modes_each)]

    def outgoing(chunk, step):
        target = lax.rem(me + step, fibers)
        return pltpu.make_async_remote_copy(
            src_ref=window(chunk, target), dst_ref=slot(chunk, me),
            send_sem=send.at[chunk, step], recv_sem=recv.at[chunk, step],
            device_id={"fiber": target}, device_id_type=MESH)

    def incoming(chunk, step):
        source = lax.rem(me - step + fibers, fibers)
        return pltpu.make_async_remote_copy(
            src_ref=slot(chunk, source), dst_ref=slot(chunk, source),
            send_sem=send.at[chunk, step], recv_sem=recv.at[chunk, step],
            device_id={"fiber": source}, device_id_type=MESH)

    def kept(chunk):
        return pltpu.make_async_copy(window(chunk, me), slot(chunk, me), own.at[chunk])

    @pl.loop(0, chunks)
    def _(chunk):
        kept(chunk).start()

        @pl.loop(1, fibers)
        def _(step):
            outgoing(chunk, step).start()

    gram[...] = jnp.zeros_like(gram)

    def written(chunk):
        return (pltpu.make_async_copy(high.at[chunk], high_ref.at[chunk], out_sem.at[0, chunk]),
                pltpu.make_async_copy(low.at[chunk], low_ref.at[chunk], out_sem.at[1, chunk]))

    @pl.loop(0, chunks)
    def _(chunk):
        def split(source):
            rows = pl.ds(pl.multiple_of(source * modes_each, modes_each), modes_each)
            values = arrived[chunk, rows].reshape(modes_each, 8 * LANES)
            top = values.astype(b16)
            high[chunk, rows, :] = top
            low[chunk, rows, :] = (values - top.astype(f32)).astype(b16)

        kept(chunk).wait()
        split(me)

        @pl.loop(1, fibers)
        def _(step):
            incoming(chunk, step).wait_recv()
            split(lax.rem(me - step + fibers, fibers))

        for copy in written(chunk):
            copy.start()
        index = packed_blocks(mode)
        for i in range(mode // 256):
            for j in range(i + 1):
                def product(a, b):
                    return lax.dot_general(a[chunk, i * 256:(i + 1) * 256, :], b[chunk, j * 256:(j + 1) * 256, :],
                                           (((1,), (1,)), ((), ())), preferred_element_type=jnp.float32)
                tile = product(high, high) + (product(high, low) + product(low, high))
                for a in range(2):
                    for b in range(2):
                        block = (2 * i + a, 2 * j + b)
                        if block in index:
                            at = index.index(block) * LANES
                            gram[at:at + LANES, :] += tile[a * LANES:(a + 1) * LANES, b * LANES:(b + 1) * LANES]

    kept_half = pl.ds(pl.multiple_of(core * half_rows, 8), half_rows)
    other_half = pl.ds(pl.multiple_of((1 - core) * half_rows, 8), half_rows)
    swap = pltpu.make_async_remote_copy(
        src_ref=gram.at[other_half], dst_ref=from_core, send_sem=core_sem.at[0], recv_sem=core_sem.at[1],
        device_id={"fiber": 2 * z + 1 - core}, device_id_type=MESH)
    swap.start()
    swap.wait()
    half[...] = gram[kept_half, :] + from_core[...]

    def part(index):
        return pl.ds(pl.multiple_of(index * part_rows, 8), part_rows)

    def to_group(step):
        target = lax.rem(group + step, groups)
        return pltpu.make_async_remote_copy(
            src_ref=half.at[part(target)], dst_ref=from_group.at[group], send_sem=group_send.at[step],
            recv_sem=group_recv.at[step], device_id={"group": target}, device_id_type=MESH)

    def of_group(step):
        source = lax.rem(group - step + groups, groups)
        return pltpu.make_async_remote_copy(
            src_ref=from_group.at[source], dst_ref=from_group.at[source], send_sem=group_send.at[step],
            recv_sem=group_recv.at[step], device_id={"group": source}, device_id_type=MESH)

    @far_first(groups)
    def _(step):
        to_group(step).start()

    from_group[group] = half[part(group), :]

    @pl.loop(1, groups)
    def _(step):
        of_group(step).wait_recv()

    sums = from_group[0]
    for index in range(1, groups):
        sums = sums + from_group[index]
    from_z[z] = sums * scale

    def to_z(step):
        target = lax.rem(z + step, zs)
        return pltpu.make_async_remote_copy(
            src_ref=from_z.at[z], dst_ref=from_z.at[z], send_sem=z_send.at[step], recv_sem=z_recv.at[step],
            device_id={"fiber": 2 * target + core}, device_id_type=MESH)

    def of_z(step):
        source = lax.rem(z - step + zs, zs)
        return pltpu.make_async_remote_copy(
            src_ref=from_z.at[source], dst_ref=from_z.at[source], send_sem=z_send.at[step], recv_sem=z_recv.at[step],
            device_id={"fiber": 2 * source + core}, device_id_type=MESH)

    @far_first(zs)
    def _(step):
        to_z(step).start()

    @pl.loop(0, chunks)
    def _(chunk):
        for copy in written(chunk):
            copy.wait()

        @pl.loop(1, fibers)
        def _(step):
            outgoing(chunk, step).wait_send()

    @pl.loop(1, zs)
    def _(step):
        of_z(step).wait_recv()

    sums = from_z[0]
    for index in range(1, zs):
        sums = sums + from_z[index]
    total[core, group] = sums

    def share(step):
        target = lax.rem(group + step, groups)
        return pltpu.make_async_remote_copy(
            src_ref=total.at[core, group], dst_ref=total.at[core, group], send_sem=last_send.at[step],
            recv_sem=last_recv.at[step], device_id={"group": target}, device_id_type=MESH)

    def shared(step):
        source = lax.rem(group - step + groups, groups)
        return pltpu.make_async_remote_copy(
            src_ref=total.at[core, source], dst_ref=total.at[core, source], send_sem=last_send.at[step],
            recv_sem=last_recv.at[step], device_id={"group": source}, device_id_type=MESH)

    @far_first(groups)
    def _(step):
        share(step).start()

    @pl.loop(1, groups)
    def _(step):
        to_group(step).wait_send()

    @pl.loop(1, zs)
    def _(step):
        to_z(step).wait_send()

    @pl.loop(1, groups)
    def _(step):
        shared(step).wait_recv()

    give = pltpu.make_async_remote_copy(
        src_ref=total.at[core], dst_ref=total.at[core], send_sem=last_core.at[0], recv_sem=last_core.at[1],
        device_id={"fiber": 2 * z + 1 - core}, device_id_type=MESH)
    take = pltpu.make_async_remote_copy(
        src_ref=total.at[1 - core], dst_ref=total.at[1 - core], send_sem=last_core.at[0], recv_sem=last_core.at[1],
        device_id={"fiber": 2 * z + 1 - core}, device_id_type=MESH)
    give.start()

    @pl.loop(1, groups)
    def _(step):
        share(step).wait_send()

    take.wait_recv()
    packed_ref[...] = total[...]
    give.wait_send()


def regroup(field_slab):
    fibers, groups = lax.axis_size("fiber"), lax.axis_size("group")
    modes_each, blocks, width = field_slab.shape
    mode, fib_cols = modes_each * fibers, width // fibers
    chunks = (blocks // 8) * (fib_cols // LANES)
    cols = 8 * LANES
    rows = len(packed_blocks(mode)) * LANES
    part_rows = rows // 2 // groups
    columns = blocks * groups * width
    dma = pltpu.SemaphoreType.DMA
    return pl.pallas_call(
        functools.partial(regroup_kernel, (fibers, groups, 1.0 / columns)),
        out_shape=(jax.ShapeDtypeStruct((chunks, mode, cols), b16), jax.ShapeDtypeStruct((chunks, mode, cols), b16),
                   jax.ShapeDtypeStruct((2, groups, part_rows, LANES), f32)),
        in_specs=[pl.BlockSpec(memory_space=pl.ANY)],
        out_specs=(pl.BlockSpec(memory_space=pl.ANY), pl.BlockSpec(memory_space=pl.ANY),
                   pl.BlockSpec(memory_space=pltpu.VMEM)),
        scratch_shapes=[
            pltpu.VMEM((chunks, mode, 8, LANES), f32), pltpu.VMEM((chunks, mode, cols), b16),
            pltpu.VMEM((chunks, mode, cols), b16), pltpu.VMEM((rows, LANES), f32),
            pltpu.VMEM((rows // 2, LANES), f32), pltpu.VMEM((rows // 2, LANES), f32),
            pltpu.VMEM((groups, part_rows, LANES), f32), pltpu.VMEM((fibers // 2, part_rows, LANES), f32),
            pltpu.VMEM((2, groups, part_rows, LANES), f32),
            dma((chunks, fibers)), dma((chunks, fibers)), dma((chunks,)), dma((2, chunks)), dma((2,)),
            dma((groups,)), dma((groups,)), dma((fibers // 2,)), dma((fibers // 2,)), dma((groups,)), dma((groups,)),
            dma((2,)),
        ],
        compiler_params=pltpu.CompilerParams(collective_id=0, has_side_effects=True, vmem_limit_bytes=40 * 2**20),
        cost_estimate=pl.CostEstimate(flops=6 * mode * mode * chunks * cols, bytes_accessed=4 * mode * chunks * cols,
                                      transcendentals=0),
    )(field_slab)


def pieces(values):
    top = values.astype(b16)
    rest = values - top.astype(f32)
    middle = rest.astype(b16)
    return top, middle, (rest - middle.astype(f32)).astype(b16)

def outer(rows):
    t, m, l = pieces(rows)
    left = jnp.concatenate([t, t, m, m, t, l], axis=0)[:, :LANES]
    right = jnp.concatenate([t, m, t, m, l, t], axis=0)
    return lax.dot_general(left, right, (((0,), (0,)), ((), ())), preferred_element_type=f32)

def inverse_lower(wide, rank, panel):
    ids = lax.broadcasted_iota(jnp.int32, (panel, LANES), 0)
    for start in range(0, rank, panel):
        rows = wide[start:start + panel, :]
        diag = [jnp.broadcast_to(rows[:, start + k:start + k + 1], (panel, LANES)) for k in range(panel)]
        parts = [rows[:, :LANES], rows[:, LANES:]]
        for j in range(panel):
            scale = lax.rsqrt(diag[j][j:j + 1, :])
            below = ids > j
            factor = jnp.where(below, diag[j] * scale, 0.0)
            keep = jnp.where(ids == j, scale, 1.0)
            def step(block):
                pivot = block[j:j + 1, :] * scale
                return block * keep - factor * pivot
            for k in range(j + 1, panel):
                diag[k] = diag[k] - factor * (diag[k][j:j + 1, :] * scale)
            parts = [step(block) for block in parts]
        rows = jnp.concatenate(parts, axis=1)
        wide[start:start + panel, :] = rows
        if start + panel < rank:
            wide[start + panel:, :] = wide[start + panel:, :] - outer(rows)[start + panel:, :]

def finish_kernel(iters, panel, packed_ref, basis_ref, high_ref, low_ref, factor_ref, core_ref, high, low, gram, wide,
                  made, in_sem, out_sem):
    mode, rank = basis_ref.shape
    chunks = high.shape[0]
    fetch = [(pltpu.make_async_copy(high_ref.at[q], high.at[q], in_sem.at[0, q]),
              pltpu.make_async_copy(low_ref.at[q], low.at[q], in_sem.at[1, q])) for q in range(chunks)]
    for pair in fetch:
        for copy in pair:
            copy.start()
    for at, (i, j) in enumerate(packed_blocks(mode)):
        block = packed_ref[at * LANES:(at + 1) * LANES, :]
        gram[i * LANES:(i + 1) * LANES, j * LANES:(j + 1) * LANES] = block
        if i != j:
            gram[j * LANES:(j + 1) * LANES, i * LANES:(i + 1) * LANES] = block.T
    subspace = basis_ref[...].T
    identity = jnp.where(lax.broadcasted_iota(jnp.int32, (rank, rank), 0)
                         == lax.broadcasted_iota(jnp.int32, (rank, rank), 1), 1.0, 0.0).astype(f32)
    for iteration in range(iters):
        images = jnp.dot(subspace, gram[...], precision=precise, preferred_element_type=f32)
        inner = lax.dot_general(images, images, (((1,), (1,)), ((), ())), precision=precise, preferred_element_type=f32)
        wide[:, :LANES] = inner
        wide[:, LANES:] = identity
        inverse_lower(wide, rank, panel)
        subspace = jnp.dot(wide[:, LANES:], images, precision=precise, preferred_element_type=f32)
    factor_ref[...] = subspace.T
    top = subspace.astype(b16)
    rest = (subspace - top.astype(f32)).astype(b16)
    both = jnp.concatenate([top, rest], axis=0)
    halves = core_ref.shape[2] // LANES
    copies = []
    for q in range(chunks):
        for copy in fetch[q]:
            copy.wait()
        first = jnp.dot(both, high[q], preferred_element_type=f32)
        second = jnp.dot(top, low[q], preferred_element_type=f32)
        made[q] = (first[:rank] + (first[rank:] + second)).reshape(rank, 8, LANES)
        row, col = q // halves * 8, q % halves * LANES
        copy = pltpu.make_async_copy(made.at[q], core_ref.at[:, row:row + 8, col:col + LANES], out_sem.at[q])
        copy.start()
        copies.append(copy)
    for copy in copies:
        copy.wait()

def finish(packed, basis, high, low, blocks, fib_cols, iters=ITERS, panel=16):
    mode, rank = basis.shape
    chunks, _, cols = high.shape
    vmem, any_ = pl.BlockSpec(memory_space=pltpu.VMEM), pl.BlockSpec(memory_space=pl.ANY)
    return pl.pallas_call(
        functools.partial(finish_kernel, iters, panel),
        out_shape=(jax.ShapeDtypeStruct((mode, rank), f32), jax.ShapeDtypeStruct((rank, blocks, fib_cols), f32)),
        in_specs=[vmem, vmem, any_, any_],
        out_specs=(vmem, any_),
        scratch_shapes=[pltpu.VMEM((chunks, mode, cols), b16), pltpu.VMEM((chunks, mode, cols), b16),
                        pltpu.VMEM((mode, mode), f32), pltpu.VMEM((rank, 2 * LANES), f32),
                        pltpu.VMEM((chunks, rank, 8, LANES), f32),
                        pltpu.SemaphoreType.DMA((2, chunks)), pltpu.SemaphoreType.DMA((chunks,))],
        compiler_params=pltpu.CompilerParams(vmem_limit_bytes=32 * 2**20),
        cost_estimate=pl.CostEstimate(flops=6 * mode * rank * chunks * cols, bytes_accessed=6 * mode * chunks * cols,
                                      transcendentals=0),
    )(packed, basis, high, low)


def on_device(field_slab, start_basis):
    fib_cols = field_slab.shape[2] // lax.axis_size("fiber")
    high, low, packed = regroup(field_slab)
    return finish(packed.reshape(-1, LANES), start_basis, high, low, field_slab.shape[1], fib_cols)


def solution(mesh):
    return jax.shard_map(
        on_device,
        mesh=mesh,
        in_specs=(P("fiber", "group", None), P()),
        out_specs=(P(), P(None, "group", "fiber")),
        check_vma=False,
    )
```

```python
import functools
import jax
import jax.numpy as jnp
from jax import lax
from jax.experimental import pallas as pl
from jax.experimental.pallas import tpu as pltpu
from jax.sharding import PartitionSpec as P

ITERS = 2
MESH = pl.DeviceIdType.MESH
precise = lax.Precision.HIGHEST
f32, b16 = jnp.float32, jnp.bfloat16

LANES = 128
PACKED = ((0, 0), (1, 0), (1, 1), (2, 0), (2, 1), (2, 2), (3, 2), (3, 3), (3, 0), (3, 1))
PORTIONS = (3, 2)


def regroup_kernel(sizes, x_ref, high_ref, low_ref, packed_ref, arrived, high, low, gram, from_core, half, from_group_a,
                   from_group_b, from_z_a, from_z_b, total, send, recv, own, out_sem, core_sem, group_send, group_recv,
                   z_send, z_recv, last_send, last_recv, last_core):
    fibers, groups, scale = sizes
    modes_each, blocks, width = x_ref.shape
    mode = modes_each * fibers
    fib_cols = width // fibers
    halves = fib_cols // LANES
    chunks = arrived.shape[0]
    me, group = lax.axis_index("fiber"), lax.axis_index("group")
    core, z = lax.rem(me, 2), lax.div(me, 2)
    zs = fibers // 2
    from_group, from_z = (from_group_a, from_group_b), (from_z_a, from_z_b)
    half_rows = half.shape[0]
    part_rows = [ref.shape[1] for ref in from_z]
    firsts = [0, groups * part_rows[0]]

    barrier = pltpu.get_barrier_semaphore()

    def far_first(count):
        def run(body):
            @pl.loop(0, count - 1)
            def _(index):
                body(lax.rem(index + count // 2 - 1, count - 1) + 1)
        return run

    @far_first(groups)
    def _(step):
        pl.semaphore_signal(barrier, inc=1, device_id={"group": lax.rem(group + step, groups)}, device_id_type=MESH)

    @far_first(fibers)
    def _(step):
        pl.semaphore_signal(barrier, inc=1, device_id={"fiber": lax.rem(me + step, fibers)}, device_id_type=MESH)

    pl.semaphore_wait(barrier, fibers + groups - 2)

    def window(chunk, owner):
        row = pl.multiple_of(lax.div(chunk, halves) * 8, 8)
        col = pl.multiple_of(owner * fib_cols + lax.rem(chunk, halves) * LANES, LANES)
        return x_ref.at[:, pl.ds(row, 8), pl.ds(col, LANES)]

    def slot(chunk, source):
        return arrived.at[chunk, pl.ds(pl.multiple_of(source * modes_each, modes_each), modes_each)]

    def outgoing(chunk, step):
        target = lax.rem(me + step, fibers)
        return pltpu.make_async_remote_copy(
            src_ref=window(chunk, target), dst_ref=slot(chunk, me),
            send_sem=send.at[chunk, step], recv_sem=recv.at[chunk, step],
            device_id={"fiber": target}, device_id_type=MESH)

    def incoming(chunk, step):
        source = lax.rem(me - step + fibers, fibers)
        return pltpu.make_async_remote_copy(
            src_ref=slot(chunk, source), dst_ref=slot(chunk, source),
            send_sem=send.at[chunk, step], recv_sem=recv.at[chunk, step],
            device_id={"fiber": source}, device_id_type=MESH)

    def kept(chunk):
        return pltpu.make_async_copy(window(chunk, me), slot(chunk, me), own.at[chunk])

    @pl.loop(0, chunks)
    def _(chunk):
        kept(chunk).start()

        @pl.loop(1, fibers)
        def _(step):
            outgoing(chunk, step).start()

    gram[...] = jnp.zeros_like(gram)

    def written(chunk):
        return (pltpu.make_async_copy(high.at[chunk], high_ref.at[chunk], out_sem.at[0, chunk]),
                pltpu.make_async_copy(low.at[chunk], low_ref.at[chunk], out_sem.at[1, chunk]))

    def arrive(chunk):
        def split(source):
            rows = pl.ds(pl.multiple_of(source * modes_each, modes_each), modes_each)
            values = arrived[chunk, rows].reshape(modes_each, 8 * LANES)
            top = values.astype(b16)
            high[chunk, rows, :] = top
            low[chunk, rows, :] = (values - top.astype(f32)).astype(b16)

        kept(chunk).wait()
        split(me)

        @pl.loop(1, fibers)
        def _(step):
            incoming(chunk, step).wait_recv()
            split(lax.rem(me - step + fibers, fibers))

        for copy in written(chunk):
            copy.start()

    def multiply(chunk, tiles):
        for i, j in tiles:
            def product(a, b):
                return lax.dot_general(a[chunk, i * 256:(i + 1) * 256, :], b[chunk, j * 256:(j + 1) * 256, :],
                                       (((1,), (1,)), ((), ())), preferred_element_type=f32)
            tile = product(high, high) + (product(high, low) + product(low, high))
            for a in range(2):
                for b in range(2):
                    block = (2 * i + a, 2 * j + b)
                    if block in PACKED:
                        at = PACKED.index(block) * LANES
                        gram[at:at + LANES, :] += tile[a * LANES:(a + 1) * LANES, b * LANES:(b + 1) * LANES]

    @pl.loop(0, chunks - 1)
    def _(chunk):
        arrive(chunk)
        multiply(chunk, ((0, 0), (1, 1), (1, 0)))

    def remote(source, target, send_sem, recv_sem, device):
        return pltpu.make_async_remote_copy(src_ref=source, dst_ref=target, send_sem=send_sem, recv_sem=recv_sem,
                                            device_id=device, device_id_type=MESH)

    def rows(first, count):
        return pl.ds(pl.multiple_of(first, 8), count)

    def whole(p):
        return rows(firsts[p], groups * part_rows[p])

    def part(p, index):
        return rows(firsts[p] + index * part_rows[p], part_rows[p])

    other = {"fiber": 2 * z + 1 - core}

    def swap(p):
        mine = rows((1 - core) * half_rows + firsts[p], groups * part_rows[p])
        return remote(gram.at[mine], from_core.at[whole(p)], core_sem.at[0, p], core_sem.at[1, p], other)

    def before(index, step, count):
        return lax.rem(index - step + count, count)

    def to_group(p, step):
        target = lax.rem(group + step, groups)
        return remote(half.at[part(p, target)], from_group[p].at[group], group_send.at[p, step], group_recv.at[p, step],
                      {"group": target})

    def of_group(p, step):
        slot = from_group[p].at[before(group, step, groups)]
        return remote(slot, slot, group_send.at[p, step], group_recv.at[p, step], {"group": before(group, step, groups)})

    def to_z(p, step):
        slot = from_z[p].at[z]
        return remote(slot, slot, z_send.at[p, step], z_recv.at[p, step], {"fiber": 2 * lax.rem(z + step, zs) + core})

    def of_z(p, step):
        slot = from_z[p].at[before(z, step, zs)]
        return remote(slot, slot, z_send.at[p, step], z_recv.at[p, step], {"fiber": 2 * before(z, step, zs) + core})

    def share(p, step):
        slot = total.at[core, part(p, group)]
        return remote(slot, slot, last_send.at[p, step], last_recv.at[p, step], {"group": lax.rem(group + step, groups)})

    def shared(p, step):
        slot = total.at[core, part(p, before(group, step, groups))]
        return remote(slot, slot, last_send.at[p, step], last_recv.at[p, step], {"group": before(group, step, groups)})

    def give(p):
        slot = total.at[core, whole(p)]
        return remote(slot, slot, last_core.at[0, p], last_core.at[1, p], other)

    def take(p):
        slot = total.at[1 - core, whole(p)]
        return remote(slot, slot, last_core.at[0, p], last_core.at[1, p], other)

    arrive(chunks - 1)
    multiply(chunks - 1, ((0, 0), (1, 1)))
    swap(0).start()
    multiply(chunks - 1, ((1, 0),))
    swap(1).start()
    for p in range(2):
        swap(p).wait_recv()
        half[whole(p), :] = gram[rows(core * half_rows + firsts[p], groups * part_rows[p]), :] + from_core[whole(p), :]
        far_first(groups)(lambda step: to_group(p, step).start())
        from_group[p][group] = half[part(p, group), :]
    for p in range(2):
        swap(p).wait_send()
        pl.loop(1, groups)(lambda step: of_group(p, step).wait_recv())
        sums = from_group[p][0]
        for index in range(1, groups):
            sums = sums + from_group[p][index]
        from_z[p][z] = sums * scale
        far_first(zs)(lambda step: to_z(p, step).start())

    @pl.loop(0, chunks)
    def _(chunk):
        for copy in written(chunk):
            copy.wait()

        @pl.loop(1, fibers)
        def _(step):
            outgoing(chunk, step).wait_send()

    for p in range(2):
        pl.loop(1, zs)(lambda step: of_z(p, step).wait_recv())
        sums = from_z[p][0]
        for index in range(1, zs):
            sums = sums + from_z[p][index]
        total[core, part(p, group), :] = sums
        far_first(groups)(lambda step: share(p, step).start())
    for p in range(2):
        pl.loop(1, groups)(lambda step: to_group(p, step).wait_send())
        pl.loop(1, zs)(lambda step: to_z(p, step).wait_send())
    for p in range(2):
        pl.loop(1, groups)(lambda step: shared(p, step).wait_recv())
        give(p).start()
    for p in range(2):
        pl.loop(1, groups)(lambda step: share(p, step).wait_send())
    for p in range(2):
        take(p).wait_recv()
    packed_ref[...] = total[...]
    for p in range(2):
        give(p).wait_send()


def regroup(field_slab):
    fibers, groups = lax.axis_size("fiber"), lax.axis_size("group")
    modes_each, blocks, width = field_slab.shape
    mode, fib_cols = modes_each * fibers, width // fibers
    chunks = (blocks // 8) * (fib_cols // LANES)
    cols = 8 * LANES
    rows = len(PACKED) * LANES
    part_a, part_b = [blocks_of * LANES // groups for blocks_of in PORTIONS]
    columns = blocks * groups * width
    dma = pltpu.SemaphoreType.DMA
    return pl.pallas_call(
        functools.partial(regroup_kernel, (fibers, groups, 1.0 / columns)),
        out_shape=(jax.ShapeDtypeStruct((chunks, mode, cols), b16), jax.ShapeDtypeStruct((chunks, mode, cols), b16),
                   jax.ShapeDtypeStruct((2, rows // 2, LANES), f32)),
        in_specs=[pl.BlockSpec(memory_space=pl.ANY)],
        out_specs=(pl.BlockSpec(memory_space=pl.ANY), pl.BlockSpec(memory_space=pl.ANY),
                   pl.BlockSpec(memory_space=pltpu.VMEM)),
        scratch_shapes=[
            pltpu.VMEM((chunks, mode, 8, LANES), f32), pltpu.VMEM((chunks, mode, cols), b16),
            pltpu.VMEM((chunks, mode, cols), b16), pltpu.VMEM((rows, LANES), f32),
            pltpu.VMEM((rows // 2, LANES), f32), pltpu.VMEM((rows // 2, LANES), f32),
            pltpu.VMEM((groups, part_a, LANES), f32), pltpu.VMEM((groups, part_b, LANES), f32),
            pltpu.VMEM((fibers // 2, part_a, LANES), f32), pltpu.VMEM((fibers // 2, part_b, LANES), f32),
            pltpu.VMEM((2, rows // 2, LANES), f32),
            dma((chunks, fibers)), dma((chunks, fibers)), dma((chunks,)), dma((2, chunks)), dma((2, 2)),
            dma((2, groups)), dma((2, groups)), dma((2, fibers // 2)), dma((2, fibers // 2)), dma((2, groups)),
            dma((2, groups)), dma((2, 2)),
        ],
        compiler_params=pltpu.CompilerParams(collective_id=0, has_side_effects=True, vmem_limit_bytes=40 * 2**20),
        cost_estimate=pl.CostEstimate(flops=6 * mode * mode * chunks * cols, bytes_accessed=4 * mode * chunks * cols,
                                      transcendentals=0),
    )(field_slab)


def pieces(values):
    top = values.astype(b16)
    rest = values - top.astype(f32)
    middle = rest.astype(b16)
    return top, middle, (rest - middle.astype(f32)).astype(b16)

def outer(rows):
    t, m, l = pieces(rows)
    left = jnp.concatenate([t, t, m, m, t, l], axis=0)[:, :LANES]
    right = jnp.concatenate([t, m, t, m, l, t], axis=0)
    return lax.dot_general(left, right, (((0,), (0,)), ((), ())), preferred_element_type=f32)

def inverse_lower(wide, rank, panel):
    ids = lax.broadcasted_iota(jnp.int32, (panel, LANES), 0)
    for start in range(0, rank, panel):
        rows = wide[start:start + panel, :]
        diag = [jnp.broadcast_to(rows[:, start + k:start + k + 1], (panel, LANES)) for k in range(panel)]
        parts = [rows[:, :LANES], rows[:, LANES:]]
        for j in range(panel):
            scale = lax.rsqrt(diag[j][j:j + 1, :])
            below = ids > j
            factor = jnp.where(below, diag[j] * scale, 0.0)
            keep = jnp.where(ids == j, scale, 1.0)
            def step(block):
                pivot = block[j:j + 1, :] * scale
                return block * keep - factor * pivot
            for k in range(j + 1, panel):
                diag[k] = diag[k] - factor * (diag[k][j:j + 1, :] * scale)
            parts = [step(block) for block in parts]
        rows = jnp.concatenate(parts, axis=1)
        wide[start:start + panel, :] = rows
        if start + panel < rank:
            wide[start + panel:, :] = wide[start + panel:, :] - outer(rows)[start + panel:, :]

def finish_kernel(iters, panel, packed_ref, basis_ref, high_ref, low_ref, factor_ref, core_ref, high, low, gram, wide,
                  made, in_sem, out_sem):
    mode, rank = basis_ref.shape
    chunks = high.shape[0]
    fetch = [(pltpu.make_async_copy(high_ref.at[q], high.at[q], in_sem.at[0, q]),
              pltpu.make_async_copy(low_ref.at[q], low.at[q], in_sem.at[1, q])) for q in range(chunks)]
    for pair in fetch:
        for copy in pair:
            copy.start()
    for at, (i, j) in enumerate(PACKED):
        block = packed_ref[at * LANES:(at + 1) * LANES, :]
        gram[i * LANES:(i + 1) * LANES, j * LANES:(j + 1) * LANES] = block
        if i != j:
            gram[j * LANES:(j + 1) * LANES, i * LANES:(i + 1) * LANES] = block.T
    subspace = basis_ref[...].T
    identity = jnp.where(lax.broadcasted_iota(jnp.int32, (rank, rank), 0)
                         == lax.broadcasted_iota(jnp.int32, (rank, rank), 1), 1.0, 0.0).astype(f32)
    for iteration in range(iters):
        images = jnp.dot(subspace, gram[...], precision=precise, preferred_element_type=f32)
        inner = lax.dot_general(images, images, (((1,), (1,)), ((), ())), precision=precise, preferred_element_type=f32)
        wide[:, :LANES] = inner
        wide[:, LANES:] = identity
        inverse_lower(wide, rank, panel)
        subspace = jnp.dot(wide[:, LANES:], images, precision=precise, preferred_element_type=f32)
    factor_ref[...] = subspace.T
    top = subspace.astype(b16)
    rest = (subspace - top.astype(f32)).astype(b16)
    both = jnp.concatenate([top, rest], axis=0)
    halves = core_ref.shape[2] // LANES
    copies = []
    for q in range(chunks):
        for copy in fetch[q]:
            copy.wait()
        first = jnp.dot(both, high[q], preferred_element_type=f32)
        second = jnp.dot(top, low[q], preferred_element_type=f32)
        made[q] = (first[:rank] + (first[rank:] + second)).reshape(rank, 8, LANES)
        row, col = q // halves * 8, q % halves * LANES
        copy = pltpu.make_async_copy(made.at[q], core_ref.at[:, row:row + 8, col:col + LANES], out_sem.at[q])
        copy.start()
        copies.append(copy)
    for copy in copies:
        copy.wait()

def finish(packed, basis, high, low, blocks, fib_cols, iters=ITERS, panel=16):
    mode, rank = basis.shape
    chunks, _, cols = high.shape
    vmem, any_ = pl.BlockSpec(memory_space=pltpu.VMEM), pl.BlockSpec(memory_space=pl.ANY)
    return pl.pallas_call(
        functools.partial(finish_kernel, iters, panel),
        out_shape=(jax.ShapeDtypeStruct((mode, rank), f32), jax.ShapeDtypeStruct((rank, blocks, fib_cols), f32)),
        in_specs=[vmem, vmem, any_, any_],
        out_specs=(vmem, any_),
        scratch_shapes=[pltpu.VMEM((chunks, mode, cols), b16), pltpu.VMEM((chunks, mode, cols), b16),
                        pltpu.VMEM((mode, mode), f32), pltpu.VMEM((rank, 2 * LANES), f32),
                        pltpu.VMEM((chunks, rank, 8, LANES), f32),
                        pltpu.SemaphoreType.DMA((2, chunks)), pltpu.SemaphoreType.DMA((chunks,))],
        compiler_params=pltpu.CompilerParams(vmem_limit_bytes=32 * 2**20),
        cost_estimate=pl.CostEstimate(flops=6 * mode * rank * chunks * cols, bytes_accessed=6 * mode * chunks * cols,
                                      transcendentals=0),
    )(packed, basis, high, low)


def on_device(field_slab, start_basis):
    fib_cols = field_slab.shape[2] // lax.axis_size("fiber")
    high, low, packed = regroup(field_slab)
    return finish(packed.reshape(-1, LANES), start_basis, high, low, field_slab.shape[1], fib_cols)


def solution(mesh):
    return jax.shard_map(
        on_device,
        mesh=mesh,
        in_specs=(P("fiber", "group", None), P()),
        out_specs=(P(), P(None, "group", "fiber")),
        check_vma=False,
    )
```

```python
import functools
import jax
import jax.numpy as jnp
from jax import lax
from jax.experimental import pallas as pl
from jax.experimental.pallas import tpu as pltpu
from jax.sharding import PartitionSpec as P

ITERS = 2
MESH = pl.DeviceIdType.MESH
precise = lax.Precision.HIGHEST
f32, b16 = jnp.float32, jnp.bfloat16

LANES = 128
PACKED = ((2, 0), (2, 1), (0, 0), (1, 0), (1, 1), (3, 0), (3, 1), (2, 2), (3, 2), (3, 3))
PORTIONS = (2, 3)


def regroup_kernel(sizes, x_ref, high_ref, low_ref, packed_ref, arrived, high, low, gram, from_core, half, from_group_a,
                   from_group_b, from_z_a, from_z_b, total, send, recv, own, out_sem, core_sem, group_send, group_recv,
                   z_send, z_recv, last_send, last_recv, last_core):
    fibers, groups, scale = sizes
    modes_each, blocks, width = x_ref.shape
    mode = modes_each * fibers
    fib_cols = width // fibers
    halves = fib_cols // LANES
    chunks = arrived.shape[0]
    me, group = lax.axis_index("fiber"), lax.axis_index("group")
    core, z = lax.rem(me, 2), lax.div(me, 2)
    zs = fibers // 2
    from_group, from_z = (from_group_a, from_group_b), (from_z_a, from_z_b)
    half_rows = half.shape[0]
    part_rows = [ref.shape[1] for ref in from_z]
    firsts = [0, groups * part_rows[0]]

    barrier = pltpu.get_barrier_semaphore()

    def far_first(count):
        def run(body):
            @pl.loop(0, count - 1)
            def _(index):
                body(lax.rem(index + count // 2 - 1, count - 1) + 1)
        return run

    @far_first(groups)
    def _(step):
        pl.semaphore_signal(barrier, inc=1, device_id={"group": lax.rem(group + step, groups)}, device_id_type=MESH)

    @far_first(fibers)
    def _(step):
        pl.semaphore_signal(barrier, inc=1, device_id={"fiber": lax.rem(me + step, fibers)}, device_id_type=MESH)

    pl.semaphore_wait(barrier, fibers + groups - 2)

    def window(chunk, owner):
        row = pl.multiple_of(lax.div(chunk, halves) * 8, 8)
        col = pl.multiple_of(owner * fib_cols + lax.rem(chunk, halves) * LANES, LANES)
        return x_ref.at[:, pl.ds(row, 8), pl.ds(col, LANES)]

    def slot(chunk, source):
        return arrived.at[chunk, pl.ds(pl.multiple_of(source * modes_each, modes_each), modes_each)]

    def outgoing(chunk, step):
        target = lax.rem(me + step, fibers)
        return pltpu.make_async_remote_copy(
            src_ref=window(chunk, target), dst_ref=slot(chunk, me),
            send_sem=send.at[chunk, step], recv_sem=recv.at[chunk, step],
            device_id={"fiber": target}, device_id_type=MESH)

    def incoming(chunk, step):
        source = lax.rem(me - step + fibers, fibers)
        return pltpu.make_async_remote_copy(
            src_ref=slot(chunk, source), dst_ref=slot(chunk, source),
            send_sem=send.at[chunk, step], recv_sem=recv.at[chunk, step],
            device_id={"fiber": source}, device_id_type=MESH)

    def kept(chunk):
        return pltpu.make_async_copy(window(chunk, me), slot(chunk, me), own.at[chunk])

    @pl.loop(0, chunks)
    def _(chunk):
        kept(chunk).start()

        @pl.loop(1, fibers)
        def _(step):
            outgoing(chunk, step).start()

    gram[...] = jnp.zeros_like(gram)

    def written(chunk):
        return (pltpu.make_async_copy(high.at[chunk], high_ref.at[chunk], out_sem.at[0, chunk]),
                pltpu.make_async_copy(low.at[chunk], low_ref.at[chunk], out_sem.at[1, chunk]))

    def arrive(chunk):
        def split(source):
            rows = pl.ds(pl.multiple_of(source * modes_each, modes_each), modes_each)
            values = arrived[chunk, rows].reshape(modes_each, 8 * LANES)
            top = values.astype(b16)
            high[chunk, rows, :] = top
            low[chunk, rows, :] = (values - top.astype(f32)).astype(b16)

        kept(chunk).wait()
        split(me)

        @pl.loop(1, fibers)
        def _(step):
            incoming(chunk, step).wait_recv()
            split(lax.rem(me - step + fibers, fibers))

        for copy in written(chunk):
            copy.start()

    def multiply(chunk, tiles):
        for i, j in tiles:
            def product(a, b):
                return lax.dot_general(a[chunk, i * 256:(i + 1) * 256, :], b[chunk, j * 256:(j + 1) * 256, :],
                                       (((1,), (1,)), ((), ())), preferred_element_type=f32)
            tile = product(high, high) + (product(high, low) + product(low, high))
            for a in range(2):
                for b in range(2):
                    block = (2 * i + a, 2 * j + b)
                    if block in PACKED:
                        at = PACKED.index(block) * LANES
                        gram[at:at + LANES, :] += tile[a * LANES:(a + 1) * LANES, b * LANES:(b + 1) * LANES]

    @pl.loop(0, chunks - 1)
    def _(chunk):
        arrive(chunk)
        multiply(chunk, ((0, 0), (1, 1), (1, 0)))

    def remote(source, target, send_sem, recv_sem, device):
        return pltpu.make_async_remote_copy(src_ref=source, dst_ref=target, send_sem=send_sem, recv_sem=recv_sem,
                                            device_id=device, device_id_type=MESH)

    def rows(first, count):
        return pl.ds(pl.multiple_of(first, 8), count)

    def whole(p):
        return rows(firsts[p], groups * part_rows[p])

    def part(p, index):
        return rows(firsts[p] + index * part_rows[p], part_rows[p])

    other = {"fiber": 2 * z + 1 - core}

    def swap(p):
        mine = rows((1 - core) * half_rows + firsts[p], groups * part_rows[p])
        return remote(gram.at[mine], from_core.at[whole(p)], core_sem.at[0, p], core_sem.at[1, p], other)

    def before(index, step, count):
        return lax.rem(index - step + count, count)

    def to_group(p, step):
        target = lax.rem(group + step, groups)
        return remote(half.at[part(p, target)], from_group[p].at[group], group_send.at[p, step], group_recv.at[p, step],
                      {"group": target})

    def of_group(p, step):
        slot = from_group[p].at[before(group, step, groups)]
        return remote(slot, slot, group_send.at[p, step], group_recv.at[p, step], {"group": before(group, step, groups)})

    def to_z(p, step):
        slot = from_z[p].at[z]
        return remote(slot, slot, z_send.at[p, step], z_recv.at[p, step], {"fiber": 2 * lax.rem(z + step, zs) + core})

    def of_z(p, step):
        slot = from_z[p].at[before(z, step, zs)]
        return remote(slot, slot, z_send.at[p, step], z_recv.at[p, step], {"fiber": 2 * before(z, step, zs) + core})

    def share(p, step):
        slot = total.at[core, part(p, group)]
        return remote(slot, slot, last_send.at[p, step], last_recv.at[p, step], {"group": lax.rem(group + step, groups)})

    def shared(p, step):
        slot = total.at[core, part(p, before(group, step, groups))]
        return remote(slot, slot, last_send.at[p, step], last_recv.at[p, step], {"group": before(group, step, groups)})

    def give(p):
        slot = total.at[core, whole(p)]
        return remote(slot, slot, last_core.at[0, p], last_core.at[1, p], other)

    def take(p):
        slot = total.at[1 - core, whole(p)]
        return remote(slot, slot, last_core.at[0, p], last_core.at[1, p], other)

    arrive(chunks - 1)
    multiply(chunks - 1, ((1, 0),))
    swap(0).start()
    multiply(chunks - 1, ((0, 0), (1, 1)))
    swap(1).start()
    for p in range(2):
        swap(p).wait_recv()
        half[whole(p), :] = gram[rows(core * half_rows + firsts[p], groups * part_rows[p]), :] + from_core[whole(p), :]
        far_first(groups)(lambda step: to_group(p, step).start())
        from_group[p][group] = half[part(p, group), :]
    for p in range(2):
        swap(p).wait_send()
        pl.loop(1, groups)(lambda step: of_group(p, step).wait_recv())
        sums = from_group[p][0]
        for index in range(1, groups):
            sums = sums + from_group[p][index]
        from_z[p][z] = sums * scale
        far_first(zs)(lambda step: to_z(p, step).start())

    @pl.loop(0, chunks)
    def _(chunk):
        for copy in written(chunk):
            copy.wait()

        @pl.loop(1, fibers)
        def _(step):
            outgoing(chunk, step).wait_send()

    for p in range(2):
        pl.loop(1, zs)(lambda step: of_z(p, step).wait_recv())
        sums = from_z[p][0]
        for index in range(1, zs):
            sums = sums + from_z[p][index]
        total[core, part(p, group), :] = sums
        far_first(groups)(lambda step: share(p, step).start())
    for p in range(2):
        pl.loop(1, groups)(lambda step: to_group(p, step).wait_send())
        pl.loop(1, zs)(lambda step: to_z(p, step).wait_send())
    for p in range(2):
        pl.loop(1, groups)(lambda step: shared(p, step).wait_recv())
        give(p).start()
    for p in range(2):
        pl.loop(1, groups)(lambda step: share(p, step).wait_send())
    for p in range(2):
        take(p).wait_recv()
    packed_ref[...] = total[...]
    for p in range(2):
        give(p).wait_send()


def regroup(field_slab):
    fibers, groups = lax.axis_size("fiber"), lax.axis_size("group")
    modes_each, blocks, width = field_slab.shape
    mode, fib_cols = modes_each * fibers, width // fibers
    chunks = (blocks // 8) * (fib_cols // LANES)
    cols = 8 * LANES
    rows = len(PACKED) * LANES
    part_a, part_b = [blocks_of * LANES // groups for blocks_of in PORTIONS]
    columns = blocks * groups * width
    dma = pltpu.SemaphoreType.DMA
    return pl.pallas_call(
        functools.partial(regroup_kernel, (fibers, groups, 1.0 / columns)),
        out_shape=(jax.ShapeDtypeStruct((chunks, mode, cols), b16), jax.ShapeDtypeStruct((chunks, mode, cols), b16),
                   jax.ShapeDtypeStruct((2, rows // 2, LANES), f32)),
        in_specs=[pl.BlockSpec(memory_space=pl.ANY)],
        out_specs=(pl.BlockSpec(memory_space=pl.ANY), pl.BlockSpec(memory_space=pl.ANY),
                   pl.BlockSpec(memory_space=pltpu.VMEM)),
        scratch_shapes=[
            pltpu.VMEM((chunks, mode, 8, LANES), f32), pltpu.VMEM((chunks, mode, cols), b16),
            pltpu.VMEM((chunks, mode, cols), b16), pltpu.VMEM((rows, LANES), f32),
            pltpu.VMEM((rows // 2, LANES), f32), pltpu.VMEM((rows // 2, LANES), f32),
            pltpu.VMEM((groups, part_a, LANES), f32), pltpu.VMEM((groups, part_b, LANES), f32),
            pltpu.VMEM((fibers // 2, part_a, LANES), f32), pltpu.VMEM((fibers // 2, part_b, LANES), f32),
            pltpu.VMEM((2, rows // 2, LANES), f32),
            dma((chunks, fibers)), dma((chunks, fibers)), dma((chunks,)), dma((2, chunks)), dma((2, 2)),
            dma((2, groups)), dma((2, groups)), dma((2, fibers // 2)), dma((2, fibers // 2)), dma((2, groups)),
            dma((2, groups)), dma((2, 2)),
        ],
        compiler_params=pltpu.CompilerParams(collective_id=0, has_side_effects=True, vmem_limit_bytes=40 * 2**20),
        cost_estimate=pl.CostEstimate(flops=6 * mode * mode * chunks * cols, bytes_accessed=4 * mode * chunks * cols,
                                      transcendentals=0),
    )(field_slab)


def pieces(values):
    top = values.astype(b16)
    rest = values - top.astype(f32)
    middle = rest.astype(b16)
    return top, middle, (rest - middle.astype(f32)).astype(b16)

def outer(rows):
    t, m, l = pieces(rows)
    left = jnp.concatenate([t, t, m, m, t, l], axis=0)[:, :LANES]
    right = jnp.concatenate([t, m, t, m, l, t], axis=0)
    return lax.dot_general(left, right, (((0,), (0,)), ((), ())), preferred_element_type=f32)

def inverse_lower(wide, rank, panel):
    left = wide[...]
    done = []
    ids = lax.broadcasted_iota(jnp.int32, (panel, LANES), 0)
    for start in range(0, rank, panel):
        rows = left[:panel, :]
        diag = [jnp.broadcast_to(rows[:, start + k:start + k + 1], (panel, LANES)) for k in range(panel)]
        parts = [rows[:, :LANES], rows[:, LANES:]]
        for j in range(panel):
            scale = lax.rsqrt(diag[j][j:j + 1, :])
            below = ids > j
            factor = jnp.where(below, diag[j] * scale, 0.0)
            keep = jnp.where(ids == j, scale, 1.0)
            def step(block):
                pivot = block[j:j + 1, :] * scale
                return block * keep - factor * pivot
            for k in range(j + 1, panel):
                diag[k] = diag[k] - factor * (diag[k][j:j + 1, :] * scale)
            parts = [step(block) for block in parts]
        rows = jnp.concatenate(parts, axis=1)
        done.append(rows[:, LANES:])
        if start + panel < rank:
            left = left[panel:, :] - outer(rows)[start + panel:, :]
    wide[:, LANES:] = jnp.concatenate(done, axis=0)


def finish_kernel(iters, panel, packed_ref, basis_ref, high_ref, low_ref, factor_ref, core_ref, high, low, gram, wide,
                  made, in_sem, out_sem):
    mode, rank = basis_ref.shape
    chunks = high.shape[0]
    fetch = [(pltpu.make_async_copy(high_ref.at[q], high.at[q], in_sem.at[0, q]),
              pltpu.make_async_copy(low_ref.at[q], low.at[q], in_sem.at[1, q])) for q in range(chunks)]
    for pair in fetch:
        for copy in pair:
            copy.start()
    for at, (i, j) in enumerate(PACKED):
        block = packed_ref[at * LANES:(at + 1) * LANES, :]
        gram[i * LANES:(i + 1) * LANES, j * LANES:(j + 1) * LANES] = block
        if i != j:
            gram[j * LANES:(j + 1) * LANES, i * LANES:(i + 1) * LANES] = block.T
    subspace = basis_ref[...].T
    identity = jnp.where(lax.broadcasted_iota(jnp.int32, (rank, rank), 0)
                         == lax.broadcasted_iota(jnp.int32, (rank, rank), 1), 1.0, 0.0).astype(f32)
    for iteration in range(iters):
        images = jnp.dot(subspace, gram[...], precision=precise, preferred_element_type=f32)
        inner = lax.dot_general(images, images, (((1,), (1,)), ((), ())), precision=precise, preferred_element_type=f32)
        wide[:, :LANES] = inner
        wide[:, LANES:] = identity
        inverse_lower(wide, rank, panel)
        subspace = jnp.dot(wide[:, LANES:], images, precision=precise, preferred_element_type=f32)
    factor_ref[...] = subspace.T
    top = subspace.astype(b16)
    rest = (subspace - top.astype(f32)).astype(b16)
    both = jnp.concatenate([top, rest], axis=0)
    halves = core_ref.shape[2] // LANES
    copies = []
    for q in range(chunks):
        for copy in fetch[q]:
            copy.wait()
        first = jnp.dot(both, high[q], preferred_element_type=f32)
        second = jnp.dot(top, low[q], preferred_element_type=f32)
        made[q] = (first[:rank] + (first[rank:] + second)).reshape(rank, 8, LANES)
        row, col = q // halves * 8, q % halves * LANES
        copy = pltpu.make_async_copy(made.at[q], core_ref.at[:, row:row + 8, col:col + LANES], out_sem.at[q])
        copy.start()
        copies.append(copy)
    for copy in copies:
        copy.wait()

def finish(packed, basis, high, low, blocks, fib_cols, iters=ITERS, panel=16):
    mode, rank = basis.shape
    chunks, _, cols = high.shape
    vmem, any_ = pl.BlockSpec(memory_space=pltpu.VMEM), pl.BlockSpec(memory_space=pl.ANY)
    return pl.pallas_call(
        functools.partial(finish_kernel, iters, panel),
        out_shape=(jax.ShapeDtypeStruct((mode, rank), f32), jax.ShapeDtypeStruct((rank, blocks, fib_cols), f32)),
        in_specs=[vmem, vmem, any_, any_],
        out_specs=(vmem, any_),
        scratch_shapes=[pltpu.VMEM((chunks, mode, cols), b16), pltpu.VMEM((chunks, mode, cols), b16),
                        pltpu.VMEM((mode, mode), f32), pltpu.VMEM((rank, 2 * LANES), f32),
                        pltpu.VMEM((chunks, rank, 8, LANES), f32),
                        pltpu.SemaphoreType.DMA((2, chunks)), pltpu.SemaphoreType.DMA((chunks,))],
        compiler_params=pltpu.CompilerParams(vmem_limit_bytes=32 * 2**20),
        cost_estimate=pl.CostEstimate(flops=6 * mode * rank * chunks * cols, bytes_accessed=6 * mode * chunks * cols,
                                      transcendentals=0),
    )(packed, basis, high, low)


def on_device(field_slab, start_basis):
    fib_cols = field_slab.shape[2] // lax.axis_size("fiber")
    high, low, packed = regroup(field_slab)
    return finish(packed.reshape(-1, LANES), start_basis, high, low, field_slab.shape[1], fib_cols)


def solution(mesh):
    return jax.shard_map(
        on_device,
        mesh=mesh,
        in_specs=(P("fiber", "group", None), P()),
        out_specs=(P(), P(None, "group", "fiber")),
        check_vma=False,
    )
```

```python
import functools
import jax
import jax.numpy as jnp
from jax import lax
from jax.experimental import pallas as pl
from jax.experimental.pallas import tpu as pltpu
from jax.sharding import PartitionSpec as P

ITERS = 2
MESH = pl.DeviceIdType.MESH
precise = lax.Precision.HIGHEST
f32, b16 = jnp.float32, jnp.bfloat16

LANES = 128
PACKED = ((0, 0), (1, 0), (1, 1), (2, 0), (2, 1), (2, 2), (3, 2), (3, 3), (3, 0), (3, 1))
PORTIONS = (3, 2)


def regroup_kernel(sizes, x_ref, high_ref, low_ref, packed_ref, arrived, high, low, gram, from_core, half, from_group_a,
                   from_group_b, from_z_a, from_z_b, total, send, recv, own, out_sem, core_sem, group_send, group_recv,
                   z_send, z_recv, last_send, last_recv, last_core):
    fibers, groups, scale = sizes
    modes_each, blocks, width = x_ref.shape
    mode = modes_each * fibers
    fib_cols = width // fibers
    halves = fib_cols // LANES
    chunks = arrived.shape[0]
    me, group = lax.axis_index("fiber"), lax.axis_index("group")
    core, z = lax.rem(me, 2), lax.div(me, 2)
    zs = fibers // 2
    from_group, from_z = (from_group_a, from_group_b), (from_z_a, from_z_b)
    half_rows = half.shape[0]
    part_rows = [ref.shape[1] for ref in from_z]
    firsts = [0, groups * part_rows[0]]

    barrier = pltpu.get_barrier_semaphore()

    def far_first(count):
        def run(body):
            @pl.loop(0, count - 1)
            def _(index):
                body(lax.rem(index + count // 2 - 1, count - 1) + 1)
        return run

    def near_first(body):
        @pl.loop(0, fibers - 1)
        def _(index):
            pair, odd = lax.div(index, 2), lax.rem(index, 2)
            body((1 - odd) * (pair + 1) + odd * (fibers - 1 - pair))

    @far_first(groups)
    def _(step):
        pl.semaphore_signal(barrier, inc=1, device_id={"group": lax.rem(group + step, groups)}, device_id_type=MESH)

    @far_first(fibers)
    def _(step):
        pl.semaphore_signal(barrier, inc=1, device_id={"fiber": lax.rem(me + step, fibers)}, device_id_type=MESH)

    pl.semaphore_wait(barrier, fibers + groups - 2)

    def window(chunk, owner):
        row = pl.multiple_of(lax.div(chunk, halves) * 8, 8)
        col = pl.multiple_of(owner * fib_cols + lax.rem(chunk, halves) * LANES, LANES)
        return x_ref.at[:, pl.ds(row, 8), pl.ds(col, LANES)]

    def slot(chunk, source):
        return arrived.at[chunk, pl.ds(pl.multiple_of(source * modes_each, modes_each), modes_each)]

    def outgoing(chunk, step):
        target = lax.rem(me + step, fibers)
        return pltpu.make_async_remote_copy(
            src_ref=window(chunk, target), dst_ref=slot(chunk, me),
            send_sem=send.at[chunk, step], recv_sem=recv.at[chunk, step],
            device_id={"fiber": target}, device_id_type=MESH)

    def incoming(chunk, step):
        source = lax.rem(me - step + fibers, fibers)
        return pltpu.make_async_remote_copy(
            src_ref=slot(chunk, source), dst_ref=slot(chunk, source),
            send_sem=send.at[chunk, step], recv_sem=recv.at[chunk, step],
            device_id={"fiber": source}, device_id_type=MESH)

    def kept(chunk):
        return pltpu.make_async_copy(window(chunk, me), slot(chunk, me), own.at[chunk])

    @pl.loop(0, chunks)
    def _(chunk):
        kept(chunk).start()

        @near_first
        def _(step):
            outgoing(chunk, step).start()

    gram[...] = jnp.zeros_like(gram)

    def written(chunk):
        return (pltpu.make_async_copy(high.at[chunk], high_ref.at[chunk], out_sem.at[0, chunk]),
                pltpu.make_async_copy(low.at[chunk], low_ref.at[chunk], out_sem.at[1, chunk]))

    def arrive(chunk):
        def split(source):
            rows = pl.ds(pl.multiple_of(source * modes_each, modes_each), modes_each)
            values = arrived[chunk, rows].reshape(modes_each, 8 * LANES)
            top = values.astype(b16)
            high[chunk, rows, :] = top
            low[chunk, rows, :] = (values - top.astype(f32)).astype(b16)

        kept(chunk).wait()
        split(me)

        @near_first
        def _(step):
            incoming(chunk, step).wait_recv()
            split(lax.rem(me - step + fibers, fibers))

        for copy in written(chunk):
            copy.start()

    def multiply(chunk, tiles):
        for i, j in tiles:
            def product(a, b):
                return lax.dot_general(a[chunk, i * 256:(i + 1) * 256, :], b[chunk, j * 256:(j + 1) * 256, :],
                                       (((1,), (1,)), ((), ())), preferred_element_type=f32)
            tile = product(high, high) + (product(high, low) + product(low, high))
            for a in range(2):
                for b in range(2):
                    block = (2 * i + a, 2 * j + b)
                    if block in PACKED:
                        at = PACKED.index(block) * LANES
                        gram[at:at + LANES, :] += tile[a * LANES:(a + 1) * LANES, b * LANES:(b + 1) * LANES]

    @pl.loop(0, chunks - 1)
    def _(chunk):
        arrive(chunk)
        multiply(chunk, ((0, 0), (1, 1), (1, 0)))

    def remote(source, target, send_sem, recv_sem, device):
        return pltpu.make_async_remote_copy(src_ref=source, dst_ref=target, send_sem=send_sem, recv_sem=recv_sem,
                                            device_id=device, device_id_type=MESH)

    def rows(first, count):
        return pl.ds(pl.multiple_of(first, 8), count)

    def whole(p):
        return rows(firsts[p], groups * part_rows[p])

    def part(p, index):
        return rows(firsts[p] + index * part_rows[p], part_rows[p])

    other = {"fiber": 2 * z + 1 - core}

    def swap(p):
        mine = rows((1 - core) * half_rows + firsts[p], groups * part_rows[p])
        return remote(gram.at[mine], from_core.at[whole(p)], core_sem.at[0, p], core_sem.at[1, p], other)

    def before(index, step, count):
        return lax.rem(index - step + count, count)

    def to_group(p, step):
        target = lax.rem(group + step, groups)
        return remote(half.at[part(p, target)], from_group[p].at[group], group_send.at[p, step], group_recv.at[p, step],
                      {"group": target})

    def of_group(p, step):
        slot = from_group[p].at[before(group, step, groups)]
        return remote(slot, slot, group_send.at[p, step], group_recv.at[p, step], {"group": before(group, step, groups)})

    def to_z(p, step):
        slot = from_z[p].at[z]
        return remote(slot, slot, z_send.at[p, step], z_recv.at[p, step], {"fiber": 2 * lax.rem(z + step, zs) + core})

    def of_z(p, step):
        slot = from_z[p].at[before(z, step, zs)]
        return remote(slot, slot, z_send.at[p, step], z_recv.at[p, step], {"fiber": 2 * before(z, step, zs) + core})

    def share(p, step):
        slot = total.at[core, part(p, group)]
        return remote(slot, slot, last_send.at[p, step], last_recv.at[p, step], {"group": lax.rem(group + step, groups)})

    def shared(p, step):
        slot = total.at[core, part(p, before(group, step, groups))]
        return remote(slot, slot, last_send.at[p, step], last_recv.at[p, step], {"group": before(group, step, groups)})

    def give(p):
        slot = total.at[core, whole(p)]
        return remote(slot, slot, last_core.at[0, p], last_core.at[1, p], other)

    def take(p):
        slot = total.at[1 - core, whole(p)]
        return remote(slot, slot, last_core.at[0, p], last_core.at[1, p], other)

    arrive(chunks - 1)
    multiply(chunks - 1, ((0, 0), (1, 1)))
    swap(0).start()
    multiply(chunks - 1, ((1, 0),))
    swap(1).start()
    for p in range(2):
        swap(p).wait_recv()
        half[whole(p), :] = gram[rows(core * half_rows + firsts[p], groups * part_rows[p]), :] + from_core[whole(p), :]
        far_first(groups)(lambda step: to_group(p, step).start())
        from_group[p][group] = half[part(p, group), :]
    for p in range(2):
        swap(p).wait_send()
        pl.loop(1, groups)(lambda step: of_group(p, step).wait_recv())
        sums = from_group[p][0]
        for index in range(1, groups):
            sums = sums + from_group[p][index]
        from_z[p][z] = sums * scale
        far_first(zs)(lambda step: to_z(p, step).start())

    @pl.loop(0, chunks)
    def _(chunk):
        for copy in written(chunk):
            copy.wait()

        @pl.loop(1, fibers)
        def _(step):
            outgoing(chunk, step).wait_send()

    for p in range(2):
        pl.loop(1, zs)(lambda step: of_z(p, step).wait_recv())
        sums = from_z[p][0]
        for index in range(1, zs):
            sums = sums + from_z[p][index]
        total[core, part(p, group), :] = sums
        far_first(groups)(lambda step: share(p, step).start())
    for p in range(2):
        pl.loop(1, groups)(lambda step: to_group(p, step).wait_send())
        pl.loop(1, zs)(lambda step: to_z(p, step).wait_send())
    for p in range(2):
        pl.loop(1, groups)(lambda step: shared(p, step).wait_recv())
        give(p).start()
    for p in range(2):
        pl.loop(1, groups)(lambda step: share(p, step).wait_send())
    for p in range(2):
        take(p).wait_recv()
    packed_ref[...] = total[...]
    for p in range(2):
        give(p).wait_send()


def regroup(field_slab):
    fibers, groups = lax.axis_size("fiber"), lax.axis_size("group")
    modes_each, blocks, width = field_slab.shape
    mode, fib_cols = modes_each * fibers, width // fibers
    chunks = (blocks // 8) * (fib_cols // LANES)
    cols = 8 * LANES
    rows = len(PACKED) * LANES
    part_a, part_b = [blocks_of * LANES // groups for blocks_of in PORTIONS]
    columns = blocks * groups * width
    dma = pltpu.SemaphoreType.DMA
    return pl.pallas_call(
        functools.partial(regroup_kernel, (fibers, groups, 1.0 / columns)),
        out_shape=(jax.ShapeDtypeStruct((chunks, mode, cols), b16), jax.ShapeDtypeStruct((chunks, mode, cols), b16),
                   jax.ShapeDtypeStruct((2, rows // 2, LANES), f32)),
        in_specs=[pl.BlockSpec(memory_space=pl.ANY)],
        out_specs=(pl.BlockSpec(memory_space=pl.ANY), pl.BlockSpec(memory_space=pl.ANY),
                   pl.BlockSpec(memory_space=pltpu.VMEM)),
        scratch_shapes=[
            pltpu.VMEM((chunks, mode, 8, LANES), f32), pltpu.VMEM((chunks, mode, cols), b16),
            pltpu.VMEM((chunks, mode, cols), b16), pltpu.VMEM((rows, LANES), f32),
            pltpu.VMEM((rows // 2, LANES), f32), pltpu.VMEM((rows // 2, LANES), f32),
            pltpu.VMEM((groups, part_a, LANES), f32), pltpu.VMEM((groups, part_b, LANES), f32),
            pltpu.VMEM((fibers // 2, part_a, LANES), f32), pltpu.VMEM((fibers // 2, part_b, LANES), f32),
            pltpu.VMEM((2, rows // 2, LANES), f32),
            dma((chunks, fibers)), dma((chunks, fibers)), dma((chunks,)), dma((2, chunks)), dma((2, 2)),
            dma((2, groups)), dma((2, groups)), dma((2, fibers // 2)), dma((2, fibers // 2)), dma((2, groups)),
            dma((2, groups)), dma((2, 2)),
        ],
        compiler_params=pltpu.CompilerParams(collective_id=0, has_side_effects=True, vmem_limit_bytes=40 * 2**20),
        cost_estimate=pl.CostEstimate(flops=6 * mode * mode * chunks * cols, bytes_accessed=4 * mode * chunks * cols,
                                      transcendentals=0),
    )(field_slab)


def pieces(values):
    top = values.astype(b16)
    rest = values - top.astype(f32)
    middle = rest.astype(b16)
    return top, middle, (rest - middle.astype(f32)).astype(b16)

def outer(rows):
    t, m, l = pieces(rows)
    left = jnp.concatenate([t, t, m, m, t, l], axis=0)[:, :LANES]
    right = jnp.concatenate([t, m, t, m, l, t], axis=0)
    return lax.dot_general(left, right, (((0,), (0,)), ((), ())), preferred_element_type=f32)

def inverse_lower(wide, rank, panel):
    ids = lax.broadcasted_iota(jnp.int32, (panel, LANES), 0)
    for start in range(0, rank, panel):
        rows = wide[start:start + panel, :]
        diag = [jnp.broadcast_to(rows[:, start + k:start + k + 1], (panel, LANES)) for k in range(panel)]
        parts = [rows[:, :LANES], rows[:, LANES:]]
        for j in range(panel):
            scale = lax.rsqrt(diag[j][j:j + 1, :])
            below = ids > j
            factor = jnp.where(below, diag[j] * scale, 0.0)
            keep = jnp.where(ids == j, scale, 1.0)
            def step(block):
                pivot = block[j:j + 1, :] * scale
                return block * keep - factor * pivot
            for k in range(j + 1, panel):
                diag[k] = diag[k] - factor * (diag[k][j:j + 1, :] * scale)
            parts = [step(block) for block in parts]
        rows = jnp.concatenate(parts, axis=1)
        wide[start:start + panel, :] = rows
        if start + panel < rank:
            wide[start + panel:, :] = wide[start + panel:, :] - outer(rows)[start + panel:, :]

def finish_kernel(iters, panel, packed_ref, basis_ref, high_ref, low_ref, factor_ref, core_ref, high, low, gram, wide,
                  made, in_sem, out_sem):
    mode, rank = basis_ref.shape
    chunks = high.shape[0]
    fetch = [(pltpu.make_async_copy(high_ref.at[q], high.at[q], in_sem.at[0, q]),
              pltpu.make_async_copy(low_ref.at[q], low.at[q], in_sem.at[1, q])) for q in range(chunks)]
    for pair in fetch:
        for copy in pair:
            copy.start()
    for at, (i, j) in enumerate(PACKED):
        block = packed_ref[at * LANES:(at + 1) * LANES, :]
        gram[i * LANES:(i + 1) * LANES, j * LANES:(j + 1) * LANES] = block
        if i != j:
            gram[j * LANES:(j + 1) * LANES, i * LANES:(i + 1) * LANES] = block.T
    subspace = basis_ref[...].T
    identity = jnp.where(lax.broadcasted_iota(jnp.int32, (rank, rank), 0)
                         == lax.broadcasted_iota(jnp.int32, (rank, rank), 1), 1.0, 0.0).astype(f32)
    for iteration in range(iters):
        images = jnp.dot(subspace, gram[...], precision=precise, preferred_element_type=f32)
        inner = lax.dot_general(images, images, (((1,), (1,)), ((), ())), precision=precise, preferred_element_type=f32)
        wide[:, :LANES] = inner
        wide[:, LANES:] = identity
        inverse_lower(wide, rank, panel)
        subspace = jnp.dot(wide[:, LANES:], images, precision=precise, preferred_element_type=f32)
    factor_ref[...] = subspace.T
    top = subspace.astype(b16)
    rest = (subspace - top.astype(f32)).astype(b16)
    both = jnp.concatenate([top, rest], axis=0)
    halves = core_ref.shape[2] // LANES
    copies = []
    for q in range(chunks):
        for copy in fetch[q]:
            copy.wait()
        first = jnp.dot(both, high[q], preferred_element_type=f32)
        second = jnp.dot(top, low[q], preferred_element_type=f32)
        made[q] = (first[:rank] + (first[rank:] + second)).reshape(rank, 8, LANES)
        row, col = q // halves * 8, q % halves * LANES
        copy = pltpu.make_async_copy(made.at[q], core_ref.at[:, row:row + 8, col:col + LANES], out_sem.at[q])
        copy.start()
        copies.append(copy)
    for copy in copies:
        copy.wait()

def finish(packed, basis, high, low, blocks, fib_cols, iters=ITERS, panel=16):
    mode, rank = basis.shape
    chunks, _, cols = high.shape
    vmem, any_ = pl.BlockSpec(memory_space=pltpu.VMEM), pl.BlockSpec(memory_space=pl.ANY)
    return pl.pallas_call(
        functools.partial(finish_kernel, iters, panel),
        out_shape=(jax.ShapeDtypeStruct((mode, rank), f32), jax.ShapeDtypeStruct((rank, blocks, fib_cols), f32)),
        in_specs=[vmem, vmem, any_, any_],
        out_specs=(vmem, any_),
        scratch_shapes=[pltpu.VMEM((chunks, mode, cols), b16), pltpu.VMEM((chunks, mode, cols), b16),
                        pltpu.VMEM((mode, mode), f32), pltpu.VMEM((rank, 2 * LANES), f32),
                        pltpu.VMEM((chunks, rank, 8, LANES), f32),
                        pltpu.SemaphoreType.DMA((2, chunks)), pltpu.SemaphoreType.DMA((chunks,))],
        compiler_params=pltpu.CompilerParams(vmem_limit_bytes=32 * 2**20),
        cost_estimate=pl.CostEstimate(flops=6 * mode * rank * chunks * cols, bytes_accessed=6 * mode * chunks * cols,
                                      transcendentals=0),
    )(packed, basis, high, low)


def on_device(field_slab, start_basis):
    fib_cols = field_slab.shape[2] // lax.axis_size("fiber")
    high, low, packed = regroup(field_slab)
    return finish(packed.reshape(-1, LANES), start_basis, high, low, field_slab.shape[1], fib_cols)


def solution(mesh):
    return jax.shard_map(
        on_device,
        mesh=mesh,
        in_specs=(P("fiber", "group", None), P()),
        out_specs=(P(), P(None, "group", "fiber")),
        check_vma=False,
    )
```
